512 devices in a mesh: bin: 64 (over x, y, z_lo), diag: 8 (over z_hi, core).
Axes of the slice: x: 4, y: 8, z: 8 (z_hi: 4, z_lo: 2; z = z_hi * 2 + z_lo), core: 2. Of those that a mesh axis runs over, the one named last changes fastest.
Arguments:
- embeddings: bfloat16 [256, 24576], P('diag', 'bin'), may hold values from -6 to 6
- projection: bfloat16 [256, 64], P('diag'), may hold values from -0.375 to 0.375
- dist_bias: float32 [32, 256], replicated, may hold values from -3 to 3
- conv_weight: bfloat16 [2, 9, 32, 32], replicated, may hold values from -0.375 to 0.375
- head_weight: float32 [32], replicated, may hold values from -1 to 1
- dilations: int32 [2], replicated, may hold values from 1 to 4, as said below
- band_limit: int32 [24576], P('bin'), may hold values from 64 to 256
- cotangent: float32 [256, 24576], P('diag', 'bin'), may hold values from -6 to 6
Outputs:
- predicted: float32 [256, 24576], P('diag', 'bin')
- grad_embed: float32 [256, 24576], P('diag', 'bin')
- grad_proj: float32 [256, 64], P('diag')
- grad_conv: float32 [2, 9, 32, 32], replicated
The draws below stay inside these ranges and needn't reach their ends.
Inputs may be any that keep to these rules, and one draw needn't show every extreme that they name: `dilations`: one of the 2 layers has dilation exactly 4.
All inputs are finite; a program needn't handle non-finite values.
Results may differ from the reference program's by a relative error of at most 0.0059.
Values may be sent and summed in bfloat16 or wider, within the bound.
No kernel may reach another device: no remote copies, remote signals or barrier semaphores. Data moves between devices by JAX's collectives and lax.ppermute only.
A program may use at most 128 MiB of HBM per device.

```python
import math
import jax
import jax.numpy as jnp
from jax import lax

BIN_DEV = 384
DIAGS = 256
CHAN = 32
EMBED = 256
MAXDIL = 4
LAYERS = 2
BINS = 24576
N_BIN = 64


def draw_dilations(key, part):
    key = jax.random.fold_in(key, 11)
    first_key, second_key = jax.random.split(key)
    position = jax.random.randint(first_key, (), 0, 2)
    others = jax.random.randint(second_key, (2,), 1, MAXDIL + 1)
    return jnp.where(jnp.arange(2) == position, MAXDIL, others).astype(jnp.int32)


def plant(array, stream_key, low, high):
    dims = array.shape
    spot = [jax.random.randint(jax.random.fold_in(stream_key, axis), (), 0, dims[axis]) for axis in range(len(dims))]
    array = array.at[tuple(spot)].set(low)
    longest = dims.index(max(dims))
    spot[longest] = (spot[longest] + 1) % dims[longest]
    return array.at[tuple(spot)].set(high)


def block_scale(stream_key, extent, cuts, smallest, high):
    level, own = 1.0, jax.random.fold_in(stream_key, 6)
    for axis_at, blocks in cuts:
        draws = jnp.exp(jax.random.uniform(jax.random.fold_in(own, axis_at), (blocks,), jnp.float32, smallest / len(cuts), high / len(cuts)))
        level = level * jnp.repeat(draws, extent[axis_at] // blocks).reshape([-1 if axis == axis_at else 1 for axis in range(len(extent))])
    return level


def centred(rng, shape, spread, most, shards=(), kind=jnp.bfloat16):
    drawn = spread * jax.random.normal(rng, shape, jnp.float32)
    if shards:
        drawn = drawn * block_scale(rng, shape, shards, -0.22, 0.18)
    return jnp.clip(drawn, -most, most).astype(kind)


def setup_inputs(seed: int = 0) -> dict:
    seeds = jax.random.split(jax.random.key(seed), 9)
    return {
        "embeddings": centred(seeds[0], (EMBED, BINS), 1.0, 6.0, ((0, 8), (1, 64))),
        "projection": centred(seeds[1], (EMBED, 2 * CHAN), EMBED ** -0.5, 0.375, ((0, 8),)),
        "dist_bias": centred(seeds[2], (CHAN, DIAGS), 0.5, 3.0, (), jnp.float32),
        "conv_weight": centred(seeds[3], (LAYERS, 9, CHAN, CHAN), (9 * CHAN) ** -0.5, 0.375),
        "head_weight": centred(seeds[4], (CHAN,), CHAN ** -0.5, 1.0, (), jnp.float32),
        "dilations": draw_dilations(jax.random.fold_in(seeds[8], 71), 0),
        "band_limit": plant(jax.random.randint(seeds[6], (BINS,), DIAGS // 4, DIAGS + 1), jax.random.fold_in(seeds[6], 1), DIAGS // 4, DIAGS).astype(jnp.int32),
        "cotangent": centred(seeds[7], (DIAGS, BINS), 1.0, 6.0, ((0, 8), (1, 64)), jnp.float32),
    }


HIGHEST = lax.Precision.HIGHEST

def skew_read(window, diag_count, row_count):
    channels = window.shape[0]
    span_len = row_count + diag_count - 1
    tiled_rows = jnp.broadcast_to(window[:, None, :], (channels, diag_count, span_len)).reshape(channels, diag_count * span_len)
    tiled_rows = jnp.pad(tiled_rows, ((0, 0), (0, diag_count)))
    return tiled_rows.reshape(channels, diag_count, span_len + 1)[:, :, :row_count]

def skew_write(values):
    channels, diag_count, row_count = values.shape
    span_len = row_count + diag_count - 1
    padded = jnp.pad(values, ((0, 0), (0, 0), (0, span_len + 1 - row_count)))
    flat_view = padded.reshape(channels, diag_count * (span_len + 1))[:, :diag_count * span_len]
    return lax.optimization_barrier(jnp.sum(flat_view.reshape(channels, diag_count, span_len), axis=1))

def tap_slice(padded, diag_start, row_start, diag_count, row_count):
    return lax.dynamic_slice(padded, (jnp.int32(0), diag_start.astype(jnp.int32), row_start.astype(jnp.int32)), (padded.shape[0], diag_count, row_count))

def conv_forward(padded, weight, dilation, diag_count, row_count, margin):
    summed = jnp.zeros((weight.shape[1], diag_count, row_count), jnp.float32)
    for kernel_tap in range(9):
        along_bin = kernel_tap // 3 - 1
        along_diag = kernel_tap % 3 - 1
        sliced = tap_slice(padded, margin + along_diag * dilation, margin + along_bin * dilation, diag_count, row_count)
        summed = summed + jnp.einsum('oc,cdi->odi', weight[kernel_tap].astype(jnp.float32), sliced.astype(jnp.float32), precision=HIGHEST)
    return summed

def conv_transpose(padded, weight, dilation, diag_count, row_count, margin):
    summed = jnp.zeros((weight.shape[2], diag_count, row_count), jnp.float32)
    for kernel_tap in range(9):
        along_bin = kernel_tap // 3 - 1
        along_diag = kernel_tap % 3 - 1
        sliced = tap_slice(padded, margin - along_diag * dilation, margin - along_bin * dilation, diag_count, row_count)
        summed = summed + jnp.einsum('oc,odi->cdi', weight[kernel_tap].astype(jnp.float32), sliced.astype(jnp.float32), precision=HIGHEST)
    return summed

def weight_grad(grad_values, padded, dilation, diag_count, row_count, margin):
    results = []
    for kernel_tap in range(9):
        along_bin = kernel_tap // 3 - 1
        along_diag = kernel_tap % 3 - 1
        sliced = tap_slice(padded, margin + along_diag * dilation, margin + along_bin * dilation, diag_count, row_count)
        results.append(jnp.einsum('odi,cdi->oc', grad_values.astype(jnp.float32), sliced.astype(jnp.float32), precision=HIGHEST))
    return jnp.stack(results)

def reference(embeddings, projection, dist_bias, conv_weight, head_weight, dilations, band_limit, cotangent):
    margin = MAXDIL
    inner = 4 * margin
    region = BIN_DEV + 8 * margin
    projected = jnp.einsum('ek,eb->kb', projection.astype(jnp.float32), embeddings.astype(jnp.float32), precision=HIGHEST)
    left_padded = jnp.pad(projected[:CHAN], ((0, 0), (inner, inner)))
    right_padded = jnp.pad(projected[CHAN:], ((0, 0), (inner, DIAGS + inner)))
    limit_padded = jnp.pad(band_limit, (inner, inner))
    cot_padded = jnp.pad(cotangent, ((0, 0), (inner, inner)))
    bias_cols = dist_bias.astype(jnp.float32)[:, :, None]
    head_vector = head_weight.astype(jnp.float32)
    diag_ids = jnp.arange(DIAGS, dtype=jnp.int32)[:, None]
    anchor = jnp.int32(0)
    dilation_one = dilations[0]
    dilation_two = dilations[1]
    weight_one = conv_weight[0]
    weight_two = conv_weight[1]

    def widened(values):
        return jnp.pad(values, ((0, 0), (margin, margin), (margin, margin)))

    def block(carried, block_index):
        wgrad_sum, grad_right = carried
        first_row = (block_index * BIN_DEV).astype(jnp.int32)
        row_ids = first_row - inner + jnp.arange(region, dtype=jnp.int32)[None, :]
        left_rows = lax.dynamic_slice(left_padded, (anchor, first_row), (CHAN, region))
        right_rows = lax.dynamic_slice(right_padded, (anchor, first_row), (CHAN, region + DIAGS - 1))
        limit_rows = lax.dynamic_slice(limit_padded, (first_row,), (region,))
        cot_rows = lax.dynamic_slice(cot_padded, (anchor, first_row), (DIAGS, region))
        inside = (row_ids >= 0) & (row_ids < BINS) & (row_ids + diag_ids < BINS)
        inside_mask = inside.astype(jnp.float32)
        counted_mask = (inside & (diag_ids < limit_rows[None, :])).astype(jnp.float32)
        tanh_zero = jnp.tanh(left_rows[:, None, :] + skew_read(right_rows, DIAGS, region) + bias_cols)
        pair_zero = (inside_mask * tanh_zero).astype(jnp.bfloat16)
        padded_zero = widened(pair_zero)
        act_one = conv_forward(padded_zero, weight_one, dilation_one, DIAGS, region, margin)
        tanh_one = jnp.tanh(act_one)
        pair_one = (inside_mask * (pair_zero.astype(jnp.float32) + tanh_one)).astype(jnp.bfloat16)
        padded_one = widened(pair_one)
        tanh_two = jnp.tanh(conv_forward(padded_one, weight_two, dilation_two, DIAGS, region, margin))
        predicted = counted_mask * jnp.einsum('c,cdi->di', head_vector, tanh_two, precision=HIGHEST)
        grad_two = ((cot_rows * counted_mask)[None, :, :] * head_vector[:, None, None] * (1.0 - tanh_two * tanh_two)).astype(jnp.bfloat16)
        wgrad_two = weight_grad(grad_two[:, :, inner:inner + BIN_DEV], padded_one[:, :, inner:inner + BIN_DEV + 2 * margin], dilation_two, DIAGS, BIN_DEV, margin)
        back_one = conv_transpose(widened(grad_two), weight_two, dilation_two, DIAGS, region, margin)
        grad_one = (back_one * inside_mask * (1.0 - tanh_one * tanh_one)).astype(jnp.bfloat16)
        wgrad_one = weight_grad(grad_one[:, :, inner:inner + BIN_DEV], padded_zero[:, :, inner:inner + BIN_DEV + 2 * margin], dilation_one, DIAGS, BIN_DEV, margin)
        back_zero = inside_mask * back_one + conv_transpose(widened(grad_one), weight_one, dilation_one, DIAGS, region, margin)
        grad_pre = (back_zero * inside_mask * (1.0 - tanh_zero * tanh_zero))[:, :, inner:inner + BIN_DEV]
        grad_left = lax.optimization_barrier(jnp.sum(grad_pre, axis=1))
        spilled = skew_write(grad_pre)
        current = lax.dynamic_slice(grad_right, (anchor, first_row), (CHAN, BIN_DEV + DIAGS - 1))
        grad_right = lax.dynamic_update_slice(grad_right, current + spilled, (anchor, first_row))
        wgrad_sum = wgrad_sum + jnp.stack([wgrad_one, wgrad_two])
        return ((wgrad_sum, grad_right), (predicted[:, inner:inner + BIN_DEV], grad_left))
    start_carry = (jnp.zeros((LAYERS, 9, CHAN, CHAN), jnp.float32), jnp.zeros((CHAN, BINS + DIAGS), jnp.float32))
    (wgrad_sum, grad_right), (pred_blocks, left_blocks) = lax.scan(block, start_carry, jnp.arange(N_BIN, dtype=jnp.int32))
    predicted = jnp.transpose(pred_blocks, (1, 0, 2)).reshape(DIAGS, BINS)
    grad_left = jnp.transpose(left_blocks, (1, 0, 2)).reshape(CHAN, BINS)
    grad_both = jnp.concatenate([grad_left, grad_right[:, :BINS]], axis=0)
    scaling = 1.0 / math.sqrt(BINS * DIAGS)
    grad_embed = jnp.einsum('ek,kb->eb', projection.astype(jnp.float32), grad_both, precision=HIGHEST)
    grad_proj = scaling * jnp.einsum('eb,kb->ek', embeddings.astype(jnp.float32), grad_both, precision=HIGHEST)
    grad_conv = scaling * wgrad_sum
    return (predicted, grad_embed, grad_proj, grad_conv)
```

```python
import functools
import math

import jax
import jax.numpy as jnp
from jax import lax
from jax.experimental import pallas as pl
from jax.experimental.pallas import tpu as pltpu
from jax.sharding import PartitionSpec as P

C = 32
M = 16
LN = 512
BF = jnp.bfloat16
F32 = jnp.float32


def _dot(a, b):
    return jnp.dot(a, b, preferred_element_type=F32)


def _dot_nt(a, b):
    return lax.dot_general(a, b, (((1,), (1,)), ((), ())), preferred_element_type=F32)


def _split(x):
    hi = x.astype(BF)
    return hi, (x - hi.astype(F32)).astype(BF)


def band_kernel(dil_ref, w_ref, wt_ref, t_ref):
    rows = lax.broadcasted_iota(jnp.int32, (256, 512), 0) >> 5
    cols = lax.broadcasted_iota(jnp.int32, (256, 512), 1) >> 5
    delta = cols - rows - 4
    spread = (
        (lax.broadcasted_iota(jnp.int32, (C, 512), 1) & 31)
        == lax.broadcasted_iota(jnp.int32, (C, 512), 0)
    ).astype(F32).astype(BF)
    for layer in range(2):
        masks = [delta == b * dil_ref[layer] for b in (-1, 0, 1)]
        for kind, ref in ((0, w_ref), (1, wt_ref)):
            for slot in range(3):
                total = jnp.zeros((256, 512), F32)
                for b in range(3):
                    along = slot if kind == 0 else 2 - slot
                    w = ref[layer, 3 * along + b]
                    wide = _dot(jnp.concatenate([w] * 8, axis=0), spread)
                    total = jnp.where(masks[b if kind == 0 else 2 - b], wide, total)
                t_ref[2 * kind + layer, :, slot * 512 : (slot + 1) * 512] = total.astype(BF)


def band_weights(dilations, conv_weight):
    return pl.pallas_call(
        band_kernel,
        out_shape=jax.ShapeDtypeStruct((4, 256, 1536), BF),
        in_specs=[
            pl.BlockSpec(memory_space=pltpu.SMEM),
            pl.BlockSpec(memory_space=pltpu.VMEM),
            pl.BlockSpec(memory_space=pltpu.VMEM),
        ],
        out_specs=pl.BlockSpec(memory_space=pltpu.VMEM),
        compiler_params=pltpu.CompilerParams(vmem_limit_bytes=32 * 2**20),
        cost_estimate=pl.CostEstimate(flops=10**9, bytes_accessed=4 * 10**6, transcendentals=0),
        name="band_weights",
    )(dilations, conv_weight, jnp.swapaxes(conv_weight, 2, 3))


def pair_kernel(
    total_bins, total_diags,
    sc_ref, own_ref, next_ref, prev_ref, bias_ref, limit_ref, head_ref, t_ref,
    proj_ref, emb_ref, embn_ref,
    pred_ref, embed_ref, sums_ref,
    x0, x1, g2, g1, d0, d1, bk, mk, vbuf, ubuf, left, gwide, acc, lsum, rsum,
):
    first_row = sc_ref[0]
    first_diag = sc_ref[1]
    s1 = sc_ref[2]
    s2 = sc_ref[3]

    lane = lax.broadcasted_iota(jnp.int32, (8, LN), 1)
    low = lax.broadcasted_iota(jnp.int32, (C, 128), 1) < 64
    bin_id = first_row + jnp.where(lane < 448, lane, lane - LN)
    bin_ok = (bin_id >= 0) & (bin_id < total_bins)

    own = own_ref[...]
    nxt = next_ref[...]
    prv = prev_ref[...]
    left[:, :384] = own[:C]
    left[:, 384:] = jnp.where(low, nxt[:C, :128], prv[:C])
    low48 = lax.broadcasted_iota(jnp.int32, (48, 128), 1) < 64
    gwide[:, :384] = own[2 * C :]
    gwide[:, 384:] = jnp.where(low48, nxt[2 * C :, :128], prv[2 * C :])
    line = jnp.concatenate([prv[C : 2 * C], own[C : 2 * C], nxt[C : 2 * C]], axis=1)
    vbuf[...] = pltpu.roll(line, 784 - first_diag, 1)[:, :640]
    ubuf[...] = pltpu.roll(line, lax.rem(912 - first_diag, 896), 1)[:, :256]

    def store3(ref, row, value, shift):
        ref[0, pl.ds(row, C), :] = pltpu.roll(value, shift, 1).astype(BF)
        ref[1, pl.ds(row, C), :] = value.astype(BF)
        ref[2, pl.ds(row, C), :] = pltpu.roll(value, LN - shift, 1).astype(BF)

    def times(value, mask):
        return (value.reshape(4, 8, value.shape[1]) * mask[None]).reshape(value.shape)

    def stage_zero(g, carry):
        vg = pltpu.roll(vbuf[...], 640 - 8 * g, 1)
        ug = pltpu.roll(ubuf[...], 256 - 8 * g, 1)
        bg = pltpu.roll(bias_ref[...], 128 - 8 * g, 1)
        for r in range(8):
            k = 8 * g + r
            diag_id = first_diag - M + k
            ok = bin_ok & (bin_id + diag_id < total_bins) & (diag_id >= 0) & (diag_id < total_diags)
            mask = ok.astype(F32)
            mk[k] = mask
            shifted = jnp.concatenate(
                [vg[:, r : r + 384], jnp.where(low, vg[:, 384 + r : 512 + r], ug[:, r : r + 128])],
                axis=1,
            )
            t = jnp.tanh(left[...] + shifted + bg[:, r : r + 1])
            row = pl.multiple_of(k * C, C)
            store3(x0, row, times(t, mask), s1)

            @pl.when((g >= 2) & (g < 6))
            def _():
                d0[pl.ds(pl.multiple_of((k - M) * C, C), C), :] = times(
                    1.0 - t[:, :384] * t[:, :384], mask[:, :384]
                )
        return carry

    lax.fori_loop(0, 8, stage_zero, 0)

    def window(ref, first, width):
        rows = pl.ds(pl.multiple_of(first * C, 256), 512)
        return jnp.concatenate([ref[a, rows, :width] for a in range(3)], axis=0)

    def stage_one(g, carry):
        t1 = jnp.tanh(_dot(t_ref[0], window(x0, 8 * g, LN)))
        for r in range(8):
            k = 4 + 8 * g + r
            mask = mk[k]
            t = t1[r * C : (r + 1) * C]
            base = x0[1, pl.ds(pl.multiple_of(k * C, C), C), :].astype(F32)
            store3(x1, pl.multiple_of((k - 4) * C, C), times(base + t, mask), s2)
            d1[pl.ds(pl.multiple_of((k - 4) * C, C), C), :] = times(1.0 - t * t, mask)
        return carry

    lax.fori_loop(0, 7, stage_one, 0)

    head = head_ref[...]
    limits = limit_ref[...]
    own_bin = first_row + lax.broadcasted_iota(jnp.int32, (8, 384), 1)
    own_row = lax.broadcasted_iota(jnp.int32, (8, 384), 0)

    def stage_two(g, carry):
        t2 = jnp.tanh(_dot(t_ref[1], window(x1, 8 * g, LN)))
        cots = gwide[pl.ds(pl.multiple_of(8 * g, 8), 8), :]
        lines = []
        for r in range(8):
            k = 8 + 8 * g + r
            t = t2[r * C : (r + 1) * C]
            value = cots[r : r + 1] * (head * (1.0 - t * t))
            store3(g2, pl.multiple_of((k - 8) * C, C), value, s2)
            lines.append(jnp.sum(head[:, :384] * t[:, :384], axis=0, keepdims=True))

        @pl.when((g >= 1) & (g < 5))
        def _():
            diag_id = first_diag + 8 * (g - 1) + own_row
            ok = (own_bin + diag_id < total_bins) & (diag_id < limits)
            pred_ref[pl.ds(pl.multiple_of(8 * (g - 1), 8), 8), :] = jnp.where(
                ok, jnp.concatenate(lines, axis=0), 0.0
            )
        return carry

    lax.fori_loop(0, 6, stage_two, 0)

    def stage_three(g, carry):
        back = _dot(t_ref[3], window(g2, 8 * g, LN))
        for r in range(8):
            k = 12 + 8 * g + r
            value = back[r * C : (r + 1) * C]
            at = pl.multiple_of((k - 12) * C, C)
            store3(g1, at, value * d1[pl.ds(pl.multiple_of((k - 4) * C, C), C), :], s1)
            bk[pl.ds(at, C), :] = times(value, mk[k])[:, :384]
        return carry

    lax.fori_loop(0, 5, stage_three, 0)

    lsum[...] = jnp.zeros_like(lsum)
    rsum[...] = jnp.zeros_like(rsum)
    acc[...] = jnp.zeros_like(acc)

    def stage_four(g, carry):
        back = _dot(t_ref[2], window(g1, 8 * g, 384))
        part = jnp.zeros((C, 384), F32)
        skew = jnp.zeros((C, LN), F32)
        for r in range(8):
            kk = 8 * g + r
            value = back[r * C : (r + 1) * C] + bk[pl.ds(pl.multiple_of((kk + 4) * C, C), C), :]
            value = value * d0[pl.ds(pl.multiple_of(kk * C, C), C), :]
            part = part + value
            wide = jnp.concatenate([value, jnp.zeros((C, 128), F32)], axis=1)
            skew = skew + (pltpu.roll(wide, r, 1) if r else wide)
        lsum[...] += part
        rsum[...] += pltpu.roll(skew, 8 * g, 1)
        grad_two = g2[1, pl.ds(pl.multiple_of((8 * g + 8) * C, C), 256), :384]
        grad_one = g1[1, pl.ds(pl.multiple_of((8 * g + 4) * C, C), 256), :384]
        for a in range(3):
            near = x0[a, pl.ds(pl.multiple_of((8 * g + 12) * C, C), 512), :384]
            acc[a] += _dot_nt(grad_one, near)
            near = x1[a, pl.ds(pl.multiple_of((8 * g + 8) * C, C), 512), :384]
            acc[3 + a] += _dot_nt(grad_two, near)
        return carry

    lax.fori_loop(0, 4, stage_four, 0)

    rows = lax.broadcasted_iota(jnp.int32, (256, 512), 0) >> 5
    cols = lax.broadcasted_iota(jnp.int32, (256, 512), 1) >> 5
    delta = cols - rows - 4
    taps = []
    for layer in range(2):
        step = (s1, s2)[layer]
        for a in range(3):
            full = acc[3 * layer + a]
            for b in range(3):
                kept = jnp.where(delta == (b - 1) * step, full, 0.0)
                kept = jnp.sum(kept.reshape(8, C, 512), axis=0)
                kept = kept[:, :128] + kept[:, 128:256] + kept[:, 256:384] + kept[:, 384:]
                kept = kept + pltpu.roll(kept, 64, 1)
                taps.append(kept + pltpu.roll(kept, 32, 1))

    right = jnp.concatenate([rsum[...], jnp.zeros((C, 128), F32)], axis=1)
    right = pltpu.roll(right, first_diag, 1)
    both = jnp.concatenate(
        [jnp.concatenate([lsum[...], jnp.zeros((C, 256), F32)], axis=1), right], axis=0
    )
    high, rest = _split(both)
    proj = proj_ref[...]
    embed_ref[:, :640] = (_dot(proj, high) + _dot(proj, rest)).astype(BF)
    embed_ref[:, 640:] = jnp.zeros((256, 128), BF)
    emb = jnp.concatenate([emb_ref[...], embn_ref[...]], axis=1)
    none = jnp.zeros((2 * C, 640), BF)
    part = _dot_nt(emb, jnp.concatenate([none, high], axis=0)) + _dot_nt(
        emb, jnp.concatenate([none, rest], axis=0)
    )
    at = lax.broadcasted_iota(jnp.int32, (64, 128), 1)
    for t in range(8):
        value = jnp.where(at < 32, jnp.concatenate(taps[2 * t : 2 * t + 2], axis=0), 0.0)
        if t == 0:
            value = jnp.where(at < 32, value, jnp.concatenate(taps[16:], axis=0))
        if t < 4:
            value = jnp.where(at < 64, value, part[64 * t : 64 * t + 64])
        sums_ref[pl.ds(t, 64, stride=8), :] = value


def pair_field(total_bins, total_diags, scalars, own, nxt, prv, bias, limits, head, bands, proj, emb, embn):
    vmem = pl.BlockSpec(memory_space=pltpu.VMEM)
    return pl.pallas_call(
        functools.partial(pair_kernel, total_bins, total_diags),
        out_shape=(
            jax.ShapeDtypeStruct((32, 384), F32),
            jax.ShapeDtypeStruct((256, 768), BF),
            jax.ShapeDtypeStruct((512, 128), F32),
        ),
        in_specs=[pl.BlockSpec(memory_space=pltpu.SMEM)] + [vmem] * 10,
        out_specs=(vmem, vmem, vmem),
        scratch_shapes=[
            pltpu.VMEM((3, 64 * C, LN), BF),
            pltpu.VMEM((3, 56 * C, LN), BF),
            pltpu.VMEM((3, 48 * C, LN), BF),
            pltpu.VMEM((3, 40 * C, LN), BF),
            pltpu.VMEM((32 * C, 384), F32),
            pltpu.VMEM((56 * C, LN), F32),
            pltpu.VMEM((40 * C, 384), F32),
            pltpu.VMEM((64, 8, LN), F32),
            pltpu.VMEM((C, 640), F32),
            pltpu.VMEM((C, 256), F32),
            pltpu.VMEM((C, LN), F32),
            pltpu.VMEM((48, LN), F32),
            pltpu.VMEM((6, 256, 512), F32),
            pltpu.VMEM((C, 384), F32),
            pltpu.VMEM((C, LN), F32),
        ],
        compiler_params=pltpu.CompilerParams(vmem_limit_bytes=56 * 2**20),
        cost_estimate=pl.CostEstimate(
            flops=12 * 10**9, bytes_accessed=5 * 10**6, transcendentals=3 * 10**6
        ),
        name="pair_field",
    )(scalars, own, nxt, prv, bias, limits, head, bands, proj, emb, embn)


def on_device(
    embeddings, projection, dist_bias, conv_weight, head_weight, dilations, band_limit, cotangent
):
    bins = lax.axis_size("bin")
    diags = lax.axis_size("diag")
    diag_dev, rows_dev = cotangent.shape
    total_bins = rows_dev * bins
    total_diags = diag_dev * diags
    bin_at = lax.axis_index("bin")
    diag_at = lax.axis_index("diag")
    first_row = bin_at * rows_dev
    first_diag = diag_at * diag_dev

    bands = band_weights(dilations, conv_weight)
    bias = lax.dynamic_slice_in_dim(jnp.pad(dist_bias, ((0, 0), (M, M + 64))), first_diag, 128, 1)
    head = jnp.broadcast_to(head_weight[:, None], (C, LN))
    limits = jnp.broadcast_to(band_limit[None, :], (8, rows_dev))
    scalars = jnp.stack([first_row, first_diag, dilations[0], dilations[1]]).astype(jnp.int32)

    row_ids = first_row + jnp.arange(rows_dev, dtype=jnp.int32)[None, :]
    diag_ids = first_diag + jnp.arange(diag_dev, dtype=jnp.int32)[:, None]
    counted = (row_ids + diag_ids < total_bins) & (diag_ids < band_limit[None, :])
    cots = jnp.where(counted, cotangent, 0.0)
    cots_bf = cots.astype(BF)
    peer = jnp.arange(diags, dtype=jnp.int32)[:, None, None]
    edge = jnp.where(
        peer > diag_at, cots_bf[None, diag_dev - 8 :], cots_bf[None, :8]
    )
    own_rows = jnp.concatenate([embeddings, projection], axis=1)
    pack = jnp.concatenate(
        [
            jnp.broadcast_to(own_rows[None], (diags,) + own_rows.shape),
            jnp.pad(edge, ((0, 0), (0, 0), (0, projection.shape[1]))),
        ],
        axis=1,
    )
    got = lax.all_to_all(pack, "diag", 0, 0)
    features = diag_dev * diags
    emb_all = got[:, :diag_dev, :rows_dev].reshape(features, rows_dev)
    proj_all = got[:, :diag_dev, rows_dev:].reshape(features, -1)
    edges = got[:, diag_dev:, :rows_dev]
    before = lax.dynamic_index_in_dim(edges, jnp.maximum(diag_at - 1, 0), 0, False)
    after = lax.dynamic_index_in_dim(edges, jnp.minimum(diag_at + 1, diags - 1), 0, False)
    before = jnp.where(diag_at > 0, before.astype(F32), 0.0)
    after = jnp.where(diag_at < diags - 1, after.astype(F32), 0.0)
    projected = lax.dot_general(
        proj_all, emb_all, (((0,), (0,)), ((), ())), preferred_element_type=F32
    )
    own = jnp.concatenate([projected, before, cots, after], axis=0)

    up = [(i, i + 1) for i in range(bins - 1)]
    down = [(i + 1, i) for i in range(bins - 1)]
    nxt = lax.ppermute(own, "bin", down)
    prv = lax.ppermute(own[:, rows_dev - 128 :], "bin", up)
    embn = lax.ppermute(emb_all[:, :256], "bin", down)

    predicted, embed_parts, sums = pair_field(
        total_bins, total_diags, scalars, own, nxt, prv, bias, limits, head, bands,
        proj_all, emb_all, embn,
    )

    shares = lax.all_to_all(sums.reshape(bins, 512 // bins, 128), "bin", 0, 0)
    share = jnp.sum(shares, axis=0)
    high = share.astype(BF)
    rest = (share - high.astype(F32)).astype(BF)
    tail = jnp.pad(jnp.concatenate([high, rest], axis=0), ((0, diag_dev - 2 * share.shape[0]), (0, 0)))
    parts = embed_parts.reshape(diags, diag_dev, 768)
    parts = jnp.concatenate(
        [parts[:, :, :640], jnp.broadcast_to(tail[None], (diags,) + tail.shape)], axis=2
    )
    parts = lax.all_to_all(parts, "diag", 0, 0)
    total = jnp.sum(parts.astype(F32), axis=0)
    incoming = lax.ppermute(total[:, rows_dev:640].astype(BF), "bin", up)
    count = share.shape[0]
    whole = total[:count, 640:] + total[count : 2 * count, 640:]
    every = lax.all_to_all(
        jnp.broadcast_to(whole[None], (bins,) + whole.shape), "bin", 0, 0
    )
    grad_embed = total[:, :rows_dev] + jnp.pad(
        incoming.astype(F32), ((0, 0), (0, rows_dev - incoming.shape[1]))
    )
    scaling = 1.0 / math.sqrt(total_bins * total_diags)
    first16 = jnp.swapaxes(every[:, :, :C], 0, 1).reshape(16, C, C)
    last2 = every[:, 0, C : 2 * C].reshape(2, C, C)
    grad_conv = scaling * jnp.concatenate([first16, last2], axis=0).reshape(2, 9, C, C)
    proj_sum = jnp.swapaxes(every[:, :4, 2 * C :], 0, 1).reshape(features, 2 * C)
    grad_proj = scaling * lax.dynamic_slice_in_dim(proj_sum, first_diag, diag_dev, 0)
    return (predicted, grad_embed, grad_proj, grad_conv)


def solution(mesh):
    return jax.shard_map(
        on_device,
        mesh=mesh,
        in_specs=(
            P("diag", "bin"),
            P("diag", None),
            P(),
            P(),
            P(),
            P(),
            P("bin"),
            P("diag", "bin"),
        ),
        out_specs=(P("diag", "bin"), P("diag", "bin"), P("diag", None), P()),
        check_vma=False,
    )
```

```python
import functools
import math

import jax
import jax.numpy as jnp
from jax import lax
from jax.experimental import pallas as pl
from jax.experimental.pallas import tpu as pltpu
from jax.sharding import PartitionSpec as P

C = 32
M = 16
LN = 512
BF = jnp.bfloat16
F32 = jnp.float32


def _dot(a, b):
    return jnp.dot(a, b, preferred_element_type=F32)


def _dot_nt(a, b):
    return lax.dot_general(a, b, (((1,), (1,)), ((), ())), preferred_element_type=F32)


def _split(x):
    hi = x.astype(BF)
    return hi, (x - hi.astype(F32)).astype(BF)


def band_kernel(dil_ref, w_ref, wt_ref, t_ref):
    rows = lax.broadcasted_iota(jnp.int32, (256, 512), 0) >> 5
    cols = lax.broadcasted_iota(jnp.int32, (256, 512), 1) >> 5
    delta = cols - rows - 4
    spread = (
        (lax.broadcasted_iota(jnp.int32, (C, 512), 1) & 31)
        == lax.broadcasted_iota(jnp.int32, (C, 512), 0)
    ).astype(F32).astype(BF)
    for layer in range(2):
        masks = [delta == b * dil_ref[layer] for b in (-1, 0, 1)]
        for kind, ref in ((0, w_ref), (1, wt_ref)):
            for slot in range(3):
                total = jnp.zeros((256, 512), F32)
                for b in range(3):
                    along = slot if kind == 0 else 2 - slot
                    w = ref[layer, 3 * along + b]
                    wide = _dot(jnp.concatenate([w] * 8, axis=0), spread)
                    total = jnp.where(masks[b if kind == 0 else 2 - b], wide, total)
                t_ref[2 * kind + layer, :, slot * 512 : (slot + 1) * 512] = total.astype(BF)


def band_weights(dilations, conv_weight):
    return pl.pallas_call(
        band_kernel,
        out_shape=jax.ShapeDtypeStruct((4, 256, 1536), BF),
        in_specs=[
            pl.BlockSpec(memory_space=pltpu.SMEM),
            pl.BlockSpec(memory_space=pltpu.VMEM),
            pl.BlockSpec(memory_space=pltpu.VMEM),
        ],
        out_specs=pl.BlockSpec(memory_space=pltpu.VMEM),
        compiler_params=pltpu.CompilerParams(vmem_limit_bytes=32 * 2**20),
        cost_estimate=pl.CostEstimate(flops=10**9, bytes_accessed=4 * 10**6, transcendentals=0),
        name="band_weights",
    )(dilations, conv_weight, jnp.swapaxes(conv_weight, 2, 3))


def pair_kernel(
    total_bins, total_diags,
    sc_ref, own_ref, next_ref, prev_ref, bias_ref, limit_ref, head_ref, t_ref, emb_ref,
    pred_ref, both_ref, spill_ref, sums_ref,
    x0, x1, g2, g1, d0, d1, bk, mk, vbuf, ubuf, left, gwide, acc, lsum, rsum,
):
    first_row = sc_ref[0]
    first_diag = sc_ref[1]
    s1 = sc_ref[2]
    s2 = sc_ref[3]

    lane = lax.broadcasted_iota(jnp.int32, (8, LN), 1)
    low = lax.broadcasted_iota(jnp.int32, (C, 128), 1) < 64
    bin_id = first_row + jnp.where(lane < 448, lane, lane - LN)
    bin_ok = (bin_id >= 0) & (bin_id < total_bins)

    own = own_ref[...]
    prv = prev_ref[...]

    def rows_of(first, count, lanes):
        return next_ref[first : first + count, lanes].astype(F32)

    every, head_half, tail_half = slice(None), slice(0, 128), slice(128, 256)
    next_right = jnp.concatenate(
        [
            rows_of(0, C, every) + rows_of(C, C, every),
            rows_of(2 * C, C, head_half) + rows_of(2 * C, C, tail_half),
        ],
        axis=1,
    )
    next_left = rows_of(3 * C, C, head_half) + rows_of(3 * C, C, tail_half)
    next_cots = rows_of(4 * C, 48, head_half)
    left[:, :384] = own[:C]
    left[:, 384:] = jnp.where(low, next_left, prv[:C])
    low48 = lax.broadcasted_iota(jnp.int32, (48, 128), 1) < 64
    gwide[:, :384] = own[2 * C :]
    gwide[:, 384:] = jnp.where(low48, next_cots, prv[2 * C :])
    line = jnp.concatenate([prv[C : 2 * C], own[C : 2 * C], next_right], axis=1)
    vbuf[...] = pltpu.roll(line, 784 - first_diag, 1)[:, :512]
    ubuf[...] = pltpu.roll(line, lax.rem(912 - first_diag, 896), 1)[:, :256]

    at = lax.broadcasted_iota(jnp.int32, (C, 128), 1)

    def columns(value):
        return [value[:, 128 * i : 128 * i + 128] for i in range(value.shape[1] // 128)]

    def store3(ref, row, value, shift):
        cols = columns(value.astype(BF))
        later = [pltpu.roll(v, shift, 1) for v in cols]
        sooner = [pltpu.roll(v, 128 - shift, 1) for v in cols]
        ref[1, pl.ds(row, C), :] = value.astype(BF)
        for i in range(4):
            here = pl.ds(128 * i, 128)
            ref[0, pl.ds(row, C), here] = jnp.where(at < shift, later[i - 1], later[i])
            ref[2, pl.ds(row, C), here] = jnp.where(
                at < 128 - shift, sooner[i], sooner[(i + 1) % 4]
            )

    def times(value, mask):
        return (value.reshape(4, 8, value.shape[1]) * mask[None]).reshape(value.shape)

    def stage_zero(g):
        for r in range(8):
            k = 8 * g + r
            diag_id = first_diag - M + k
            ok = bin_ok & (bin_id + diag_id < total_bins) & (diag_id >= 0) & (diag_id < total_diags)
            mask = ok.astype(F32)
            mk[k] = mask
            by = (128 - k) % 128
            v = [pltpu.roll(vbuf[:, 128 * i : 128 * i + 128], by, 1) for i in range(4)]
            u = [pltpu.roll(ubuf[:, 128 * i : 128 * i + 128], by, 1) for i in range(2)]
            here = at < 128 - k
            shifted = jnp.concatenate(
                [jnp.where(here, v[i], v[i + 1]) for i in range(3)]
                + [jnp.where(low, v[3], jnp.where(here, u[0], u[1]))],
                axis=1,
            )
            t = jnp.tanh(left[...] + shifted + bias_ref[:, k : k + 1])
            row = k * C
            store3(x0, row, times(t, mask), s1)
            d0[pl.ds(row, C), :] = times(1.0 - t[:, :384] * t[:, :384], mask[:, :384])


    def window(ref, first, width):
        rows = pl.ds(first * C, 512)
        return jnp.concatenate([ref[a, rows, :width] for a in range(3)], axis=0)

    def stage_one(g):
        t1 = jnp.tanh(_dot(t_ref[0], window(x0, 8 * g, LN)))
        for r in range(8):
            k = 4 + 8 * g + r
            mask = mk[k]
            t = t1[r * C : (r + 1) * C]
            base = x0[1, pl.ds(k * C, C), :].astype(F32)
            store3(x1, (k - 4) * C, times(base + t, mask), s2)
            d1[pl.ds((k - 4) * C, C), :] = times(1.0 - t * t, mask)


    head = jnp.broadcast_to(head_ref[...], (C, LN))
    limits = limit_ref[...]
    own_bin = first_row + lax.broadcasted_iota(jnp.int32, (8, 384), 1)
    own_row = lax.broadcasted_iota(jnp.int32, (8, 384), 0)

    def stage_two(g):
        t2 = jnp.tanh(_dot(t_ref[1], window(x1, 8 * g, LN)))
        cots = gwide[pl.ds(8 * g, 8), :]
        lines = []
        for r in range(8):
            k = 8 + 8 * g + r
            t = t2[r * C : (r + 1) * C]
            value = cots[r : r + 1] * (head * (1.0 - t * t))
            store3(g2, (k - 8) * C, value, s2)
            lines.append(jnp.sum(head[:, :384] * t[:, :384], axis=0, keepdims=True))

        if 1 <= g < 5:
            diag_id = first_diag + 8 * (g - 1) + own_row
            ok = (own_bin + diag_id < total_bins) & (diag_id < limits)
            pred_ref[pl.ds(8 * (g - 1), 8), :] = jnp.where(
                ok, jnp.concatenate(lines, axis=0), 0.0
            )


    def stage_three(g):
        back = _dot(t_ref[3], window(g2, 8 * g, LN))
        for r in range(8):
            k = 12 + 8 * g + r
            value = back[r * C : (r + 1) * C]
            at = (k - 12) * C
            store3(g1, at, value * d1[pl.ds((k - 4) * C, C), :], s1)
            bk[pl.ds(at, C), :] = times(value, mk[k])[:, :384]


    lsum[...] = jnp.zeros_like(lsum)
    rsum[...] = jnp.zeros_like(rsum)
    acc[...] = jnp.zeros_like(acc)

    def stage_four(g):
        back = _dot(t_ref[2], window(g1, 8 * g, 384))
        part = jnp.zeros((C, 384), F32)
        skew = jnp.zeros((C, LN), F32)
        for r in range(8):
            kk = 8 * g + r
            value = back[r * C : (r + 1) * C] + bk[pl.ds((kk + 4) * C, C), :]
            value = value * d0[pl.ds((kk + M) * C, C), :]
            part = part + value
            wide = jnp.concatenate([value, jnp.zeros((C, 128), F32)], axis=1)
            skew = skew + (pltpu.roll(wide, r, 1) if r else wide)
        lsum[...] += part
        rsum[...] += pltpu.roll(skew, 8 * g, 1)
        grad_two = g2[1, pl.ds((8 * g + 8) * C, 256), :384]
        grad_one = g1[1, pl.ds((8 * g + 4) * C, 256), :384]
        for a in range(3):
            near = x0[a, pl.ds((8 * g + 12) * C, 512), :384]
            acc[a] += _dot_nt(grad_one, near)
            near = x1[a, pl.ds((8 * g + 8) * C, 512), :384]
            acc[3 + a] += _dot_nt(grad_two, near)


    stages = ((stage_zero, 8), (stage_one, 7), (stage_two, 6), (stage_three, 5), (stage_four, 4))
    for stage, groups in stages:
        for g in range(groups):
            stage(g)

    rows = lax.broadcasted_iota(jnp.int32, (256, 512), 0) >> 5
    cols = lax.broadcasted_iota(jnp.int32, (256, 512), 1) >> 5
    delta = cols - rows - 4
    taps = []
    for layer in range(2):
        step = (s1, s2)[layer]
        for a in range(3):
            full = acc[3 * layer + a]
            for b in range(3):
                kept = jnp.where(delta == (b - 1) * step, full, 0.0)
                kept = jnp.sum(kept.reshape(8, C, 512), axis=0)
                kept = kept[:, :128] + kept[:, 128:256] + kept[:, 256:384] + kept[:, 384:]
                kept = kept + pltpu.roll(kept, 64, 1)
                taps.append(kept + pltpu.roll(kept, 32, 1))

    right = jnp.concatenate([rsum[...], jnp.zeros((C, 128), F32)], axis=1)
    right = pltpu.roll(right, first_diag, 1)
    both_ref[:C] = lsum[...]
    both_ref[C:] = right[:, :384]
    spill_ref[...] = right[:, 384:].astype(BF)
    both = jnp.concatenate(
        [jnp.concatenate([lsum[...], jnp.zeros((C, 256), F32)], axis=1), right], axis=0
    )
    none = jnp.zeros((2 * C, 640), BF)
    high, rest = _split(both)
    emb = jnp.concatenate([emb_ref[...], next_ref[4 * C + 48 :]], axis=1)
    part = _dot_nt(emb, jnp.concatenate([none, high], axis=0)) + _dot_nt(
        emb, jnp.concatenate([none, rest], axis=0)
    )
    for t in range(16):
        value = jnp.where(at < 32, taps[t], 0.0)
        if t < 2:
            value = jnp.where(at < 32, value, taps[16 + t])
        if t < 8:
            value = jnp.where(at < 64, value, part[C * t : C * t + C])
        sums_ref[C * t : C * t + C] = value


def pair_field(total_bins, total_diags, *operands):
    vmem = pl.BlockSpec(memory_space=pltpu.VMEM)
    return pl.pallas_call(
        functools.partial(pair_kernel, total_bins, total_diags),
        out_shape=(
            jax.ShapeDtypeStruct((32, 384), F32),
            jax.ShapeDtypeStruct((2 * C, 384), F32),
            jax.ShapeDtypeStruct((C, 256), BF),
            jax.ShapeDtypeStruct((512, 128), F32),
        ),
        in_specs=[pl.BlockSpec(memory_space=pltpu.SMEM)] + [vmem] * 8,
        out_specs=(vmem,) * 4,
        scratch_shapes=[
            pltpu.VMEM((3, 64 * C, LN), BF),
            pltpu.VMEM((3, 56 * C, LN), BF),
            pltpu.VMEM((3, 48 * C, LN), BF),
            pltpu.VMEM((3, 40 * C, LN), BF),
            pltpu.VMEM((64 * C, 384), F32),
            pltpu.VMEM((56 * C, LN), F32),
            pltpu.VMEM((40 * C, 384), F32),
            pltpu.VMEM((64, 8, LN), F32),
            pltpu.VMEM((C, 512), F32),
            pltpu.VMEM((C, 256), F32),
            pltpu.VMEM((C, LN), F32),
            pltpu.VMEM((48, LN), F32),
            pltpu.VMEM((6, 256, 512), F32),
            pltpu.VMEM((C, 384), F32),
            pltpu.VMEM((C, LN), F32),
        ],
        compiler_params=pltpu.CompilerParams(vmem_limit_bytes=56 * 2**20),
        cost_estimate=pl.CostEstimate(
            flops=12 * 10**9, bytes_accessed=5 * 10**6, transcendentals=3 * 10**6
        ),
        name="pair_field",
    )(*operands)


def on_device(
    embeddings, projection, dist_bias, conv_weight, head_weight, dilations, band_limit, cotangent
):
    bins = lax.axis_size("bin")
    diags = lax.axis_size("diag")
    diag_dev, rows_dev = cotangent.shape
    total_bins = rows_dev * bins
    total_diags = diag_dev * diags
    bin_at = lax.axis_index("bin")
    diag_at = lax.axis_index("diag")
    first_row = bin_at * rows_dev
    first_diag = diag_at * diag_dev

    bands = band_weights(dilations, conv_weight)
    bias = lax.dynamic_slice_in_dim(jnp.pad(dist_bias, ((0, 0), (M, M + 64))), first_diag, 128, 1)
    scalars = jnp.stack([first_row, first_diag, dilations[0], dilations[1]]).astype(jnp.int32)

    row_ids = first_row + jnp.arange(rows_dev, dtype=jnp.int32)[None, :]
    diag_ids = first_diag + jnp.arange(diag_dev, dtype=jnp.int32)[:, None]
    counted = (row_ids + diag_ids < total_bins) & (diag_ids < band_limit[None, :])
    cots = jnp.where(counted, cotangent, 0.0)
    cots_bf = cots.astype(BF)
    peer = jnp.arange(diags, dtype=jnp.int32)[:, None, None]
    edge = jnp.where(
        peer > diag_at, cots_bf[None, diag_dev - 8 :], cots_bf[None, :8]
    )
    columns = projection.shape[1]
    quarter = diag_dev // 4
    flat = jnp.concatenate([projection[quarter * i : quarter * (i + 1)] for i in range(4)], axis=1)
    flat = jnp.pad(flat, ((0, 0), (0, rows_dev - 4 * columns)))
    pack = jnp.concatenate(
        [
            jnp.broadcast_to(embeddings[None], (diags,) + embeddings.shape),
            edge,
            jnp.broadcast_to(flat[None], (diags,) + flat.shape),
        ],
        axis=1,
    )
    got = lax.all_to_all(pack, "diag", 0, 0)
    got, bands, bias = lax.optimization_barrier((got, bands, bias))
    features = diag_dev * diags
    emb_all = got[:, :diag_dev].reshape(features, rows_dev)
    flat = got[:, diag_dev + 8 :]
    proj_all = jnp.concatenate(
        [flat[:, :, columns * i : columns * (i + 1)] for i in range(4)], axis=1
    ).reshape(features, columns)
    edges = got[:, diag_dev : diag_dev + 8]
    before = lax.dynamic_index_in_dim(edges, jnp.maximum(diag_at - 1, 0), 0, False)
    after = lax.dynamic_index_in_dim(edges, jnp.minimum(diag_at + 1, diags - 1), 0, False)
    before = jnp.where(diag_at > 0, before.astype(F32), 0.0)
    after = jnp.where(diag_at < diags - 1, after.astype(F32), 0.0)
    projected = lax.dot_general(
        proj_all, emb_all, (((0,), (0,)), ((), ())), preferred_element_type=F32
    )
    own = jnp.concatenate([projected, before, cots, after], axis=0)

    up = [(i, i + 1) for i in range(bins - 1)]
    down = [(i + 1, i) for i in range(bins - 1)]
    high, rest = _split(projected)
    first = jnp.concatenate(
        [
            high[C:, :256],
            rest[C:, :256],
            jnp.concatenate([high[C:, 256:], rest[C:, 256:]], axis=1),
            jnp.concatenate([high[:C, :128], rest[:C, :128]], axis=1),
            own[2 * C :, :256].astype(BF),
            emb_all[:, :256],
        ],
        axis=0,
    )
    nxt = lax.ppermute(first, "bin", down)
    prv = lax.ppermute(own[:, rows_dev - 128 :], "bin", up)

    predicted, both, spill, sums = pair_field(
        total_bins, total_diags, scalars, own, nxt, prv, bias, band_limit[None, :],
        head_weight[:, None], bands, emb_all,
    )

    spill = lax.ppermute(spill, "bin", up)
    shares = lax.all_to_all(sums.reshape(bins, 512 // bins, 128), "bin", 0, 0)
    both = both + jnp.pad(spill.astype(F32), ((C, 0), (0, rows_dev - spill.shape[1])))
    high, rest = _split(both)
    parts = _dot(
        jnp.concatenate([proj_all, proj_all], axis=1), jnp.concatenate([high, rest], axis=0)
    ).astype(BF).reshape(diags, diag_dev, rows_dev)
    share = jnp.sum(shares, axis=0)
    high, rest = _split(share)
    count = share.shape[0]
    tail = jnp.pad(jnp.concatenate([high, rest], axis=0), ((0, diag_dev - 2 * count), (0, 0)))
    parts = jnp.concatenate(
        [parts, jnp.broadcast_to(tail[None], (diags,) + tail.shape)], axis=2
    )
    total = jnp.sum(lax.all_to_all(parts, "diag", 0, 0).astype(F32), axis=0)
    grad_embed = total[:, :rows_dev]
    whole = total[:count, rows_dev:] + total[count : 2 * count, rows_dev:]
    every = lax.all_to_all(
        jnp.broadcast_to(whole[None], (bins,) + whole.shape), "bin", 0, 0
    ).reshape(bins * count, 128)
    scaling = 1.0 / math.sqrt(total_bins * total_diags)
    grad_conv = scaling * jnp.concatenate(
        [every[:, :C].reshape(16, C, C), every[: 2 * C, C : 2 * C].reshape(2, C, C)], axis=0
    ).reshape(2, 9, C, C)
    grad_proj = scaling * lax.dynamic_slice(
        every, (first_diag, 2 * C), (diag_dev, 2 * C)
    )
    return (predicted, grad_embed, grad_proj, grad_conv)


def solution(mesh):
    return jax.shard_map(
        on_device,
        mesh=mesh,
        in_specs=(
            P("diag", "bin"),
            P("diag", None),
            P(),
            P(),
            P(),
            P(),
            P("bin"),
            P("diag", "bin"),
        ),
        out_specs=(P("diag", "bin"), P("diag", "bin"), P("diag", None), P()),
        check_vma=False,
    )
```

```python
import functools
import math

import jax
import jax.numpy as jnp
from jax import lax
from jax.experimental import pallas as pl
from jax.experimental.pallas import tpu as pltpu
from jax.sharding import PartitionSpec as P

C = 32
M = 16
LN = 512
BF = jnp.bfloat16
F32 = jnp.float32


def _dot(a, b):
    return jnp.dot(a, b, preferred_element_type=F32)


def _dot_nt(a, b):
    return lax.dot_general(a, b, (((1,), (1,)), ((), ())), preferred_element_type=F32)


def _split(x):
    hi = x.astype(BF)
    return hi, (x - hi.astype(F32)).astype(BF)


def band_kernel(dil_ref, w_ref, t_ref):
    spread = (
        (lax.broadcasted_iota(jnp.int32, (C, 512), 1) & 31)
        == lax.broadcasted_iota(jnp.int32, (C, 512), 0)
    ).astype(F32).astype(BF)
    offset = (lax.broadcasted_iota(jnp.int32, (C, 512), 1) >> 5) - 4
    for layer in range(2):
        step = dil_ref[layer]
        for kind in range(2):
            for slot in range(3):
                wide = []
                for b in range(3):
                    if kind == 0:
                        wide.append(_dot(w_ref[layer, 3 * slot + b], spread))
                    else:
                        w = w_ref[layer, 3 * (2 - slot) + 2 - b]
                        wide.append(
                            lax.dot_general(
                                w, spread, (((0,), (0,)), ((), ())), preferred_element_type=F32
                            )
                        )
                for j in range(8):
                    value = jnp.zeros((C, 512), F32)
                    for b in range(3):
                        value = jnp.where(offset == j + (b - 1) * step, wide[b], value)
                    t_ref[2 * kind + layer, C * j : C * j + C, 512 * slot : 512 * slot + 512] = (
                        value.astype(BF)
                    )


def band_weights(dilations, conv_weight):
    return pl.pallas_call(
        band_kernel,
        out_shape=jax.ShapeDtypeStruct((4, 256, 1536), BF),
        in_specs=[
            pl.BlockSpec(memory_space=pltpu.SMEM),
            pl.BlockSpec(memory_space=pltpu.VMEM),
        ],
        out_specs=pl.BlockSpec(memory_space=pltpu.VMEM),
        compiler_params=pltpu.CompilerParams(vmem_limit_bytes=32 * 2**20),
        cost_estimate=pl.CostEstimate(flops=10**9, bytes_accessed=4 * 10**6, transcendentals=0),
        name="band_weights",
    )(dilations, conv_weight)


def prepare_kernel(total_bins, emb_ref, proj_ref, cot_ref, limit_ref, pack_ref, cots_ref):
    diag_dev, rows_dev = cot_ref.shape
    diag_at = lax.axis_index("diag")
    first_row = lax.axis_index("bin") * rows_dev
    shape = (diag_dev, rows_dev)
    bin_id = first_row + lax.broadcasted_iota(jnp.int32, shape, 1)
    diag_id = diag_at * diag_dev + lax.broadcasted_iota(jnp.int32, shape, 0)
    counted = (bin_id + diag_id < total_bins) & (diag_id < limit_ref[...][None, :])
    cots = jnp.where(counted, cot_ref[...], 0.0)
    cots_ref[...] = cots
    columns = proj_ref.shape[1]
    quarter = diag_dev // 4
    proj = proj_ref[...].astype(F32)
    flat = jnp.concatenate(
        [proj[quarter * i : quarter * (i + 1)] for i in range(4)]
        + [jnp.zeros((quarter, rows_dev - 4 * columns), F32)],
        axis=1,
    )
    last = jnp.concatenate([cots[diag_dev - 8 :], flat], axis=0)
    first = jnp.concatenate([cots[:8], flat], axis=0)
    for peer in range(pack_ref.shape[0]):
        pack_ref[peer, :diag_dev] = emb_ref[...]
        pack_ref[peer, diag_dev:] = jnp.where(peer > diag_at, last, first).astype(BF)


def prepare(total_bins, diags, *operands):
    diag_dev, rows_dev = operands[0].shape
    vmem = pl.BlockSpec(memory_space=pltpu.VMEM)
    return pl.pallas_call(
        functools.partial(prepare_kernel, total_bins),
        out_shape=(
            jax.ShapeDtypeStruct((diags, diag_dev + 16, rows_dev), BF),
            jax.ShapeDtypeStruct((diag_dev, rows_dev), F32),
        ),
        in_specs=[vmem] * 4,
        out_specs=(vmem, vmem),
        compiler_params=pltpu.CompilerParams(vmem_limit_bytes=16 * 2**20),
        name="prepare",
    )(*operands)


def pair_kernel(
    total_bins, total_diags,
    dil_ref, head_ref, own_ref, next_ref, prev_ref, bias_ref, limit_ref, t_ref, emb_ref,
    pred_ref, both_ref, spill_ref, sums_ref,
    x0, x1, g2, g1, d0, d1, bk, mk, vbuf, ubuf, left, gwide, acc, lsum, rsum,
):
    first_row = lax.axis_index("bin") * 384
    first_diag = lax.axis_index("diag") * 32
    s1 = dil_ref[0]
    s2 = dil_ref[1]

    lane = lax.broadcasted_iota(jnp.int32, (8, LN), 1)
    low = lax.broadcasted_iota(jnp.int32, (C, 128), 1) < 64
    bin_id = first_row + jnp.where(lane < 448, lane, lane - LN)
    bin_ok = (bin_id >= 0) & (bin_id < total_bins)

    own = own_ref[...]
    prv = prev_ref[...]

    def rows_of(first, count, lanes):
        return next_ref[first : first + count, lanes].astype(F32)

    every, head_half, tail_half = slice(None), slice(0, 128), slice(128, 256)
    next_right = jnp.concatenate(
        [
            rows_of(0, C, every) + rows_of(C, C, every),
            rows_of(2 * C, C, head_half) + rows_of(2 * C, C, tail_half),
        ],
        axis=1,
    )
    next_left = rows_of(3 * C, C, head_half) + rows_of(3 * C, C, tail_half)
    next_cots = rows_of(4 * C, 48, head_half)
    left[:, :384] = own[:C]
    left[:, 384:] = jnp.where(low, next_left, prv[:C])
    low48 = lax.broadcasted_iota(jnp.int32, (48, 128), 1) < 64
    gwide[:, :384] = own[2 * C :]
    gwide[:, 384:] = jnp.where(low48, next_cots, prv[2 * C :])
    line = jnp.concatenate([prv[C : 2 * C], own[C : 2 * C], next_right], axis=1)
    bias = pltpu.roll(bias_ref[...], lax.rem(256 + M - first_diag, 256), 1)
    vbuf[...] = pltpu.roll(line, 784 - first_diag, 1)[:, :512]
    ubuf[...] = pltpu.roll(line, lax.rem(912 - first_diag, 896), 1)[:, :256]

    at = lax.broadcasted_iota(jnp.int32, (C, 128), 1)

    def spread(ref, rows, shift):
        for row in rows:
            cols = [ref[1, row : row + C, 128 * i : 128 * i + 128] for i in range(4)]
            later = [pltpu.roll(v, shift, 1) for v in cols]
            sooner = [pltpu.roll(v, 128 - shift, 1) for v in cols]
            for i in range(4):
                here = slice(128 * i, 128 * i + 128)
                ref[0, row : row + C, here] = jnp.where(at < shift, later[i - 1], later[i])
                ref[2, row : row + C, here] = jnp.where(
                    at < 128 - shift, sooner[i], sooner[(i + 1) % 4]
                )

    def times(value, mask):
        return (value.reshape(4, 8, value.shape[1]) * mask[None]).reshape(value.shape)

    def stage_zero(g):
        for r in range(8):
            k = 8 * g + r
            diag_id = first_diag - M + k
            ok = bin_ok & (bin_id + diag_id < total_bins) & (diag_id >= 0) & (diag_id < total_diags)
            mask = ok.astype(F32)
            mk[k] = mask
            by = (128 - k) % 128
            v = [pltpu.roll(vbuf[:, 128 * i : 128 * i + 128], by, 1) for i in range(4)]
            u = [pltpu.roll(ubuf[:, 128 * i : 128 * i + 128], by, 1) for i in range(2)]
            here = at < 128 - k
            shifted = jnp.concatenate(
                [jnp.where(here, v[i], v[i + 1]) for i in range(3)]
                + [jnp.where(low, v[3], jnp.where(here, u[0], u[1]))],
                axis=1,
            )
            t = jnp.tanh(left[...] + shifted + bias[:, k : k + 1])
            row = k * C
            x0[1, row : row + C] = times(t, mask).astype(BF)
            d0[pl.ds(row, C), :] = times(1.0 - t[:, :384] * t[:, :384], mask[:, :384])
        spread(x0, range(8 * g * C, (8 * g + 8) * C, C), s1)


    def window(ref, first, width):
        rows = pl.ds(first * C, 512)
        return jnp.concatenate([ref[a, rows, :width] for a in range(3)], axis=0)

    def stage_one(g):
        t1 = jnp.tanh(_dot(t_ref[0], window(x0, 8 * g, LN)))
        for r in range(8):
            k = 4 + 8 * g + r
            mask = mk[k]
            t = t1[r * C : (r + 1) * C]
            base = x0[1, pl.ds(k * C, C), :].astype(F32)
            x1[1, pl.ds((k - 4) * C, C), :] = times(base + t, mask).astype(BF)
            d1[pl.ds((k - 4) * C, C), :] = times(1.0 - t * t, mask)
        spread(x1, range(8 * g * C, (8 * g + 8) * C, C), s2)


    head = jnp.concatenate([jnp.full((1, LN), head_ref[c], F32) for c in range(C)], axis=0)
    limits = limit_ref[...][None, :]
    own_bin = first_row + lax.broadcasted_iota(jnp.int32, (8, 384), 1)
    own_row = lax.broadcasted_iota(jnp.int32, (8, 384), 0)

    def stage_two(g):
        t2 = jnp.tanh(_dot(t_ref[1], window(x1, 8 * g, LN)))
        cots = gwide[pl.ds(8 * g, 8), :]
        lines = []
        for r in range(8):
            k = 8 + 8 * g + r
            t = t2[r * C : (r + 1) * C]
            value = cots[r : r + 1] * (head * (1.0 - t * t))
            g2[1, pl.ds((k - 8) * C, C), :] = value.astype(BF)
            lines.append(jnp.sum(head[:, :384] * t[:, :384], axis=0, keepdims=True))
        spread(g2, range(8 * g * C, (8 * g + 8) * C, C), s2)

        if 1 <= g < 5:
            diag_id = first_diag + 8 * (g - 1) + own_row
            ok = (own_bin + diag_id < total_bins) & (diag_id < limits)
            pred_ref[pl.ds(8 * (g - 1), 8), :] = jnp.where(
                ok, jnp.concatenate(lines, axis=0), 0.0
            )


    def stage_three(g):
        back = _dot(t_ref[3], window(g2, 8 * g, LN))
        for r in range(8):
            k = 12 + 8 * g + r
            value = back[r * C : (r + 1) * C]
            at = (k - 12) * C
            g1[1, pl.ds(at, C), :] = (value * d1[pl.ds((k - 4) * C, C), :]).astype(BF)
            bk[pl.ds(at, C), :] = times(value, mk[k])[:, :384]
        spread(g1, range(8 * g * C, (8 * g + 8) * C, C), s1)


    lsum[...] = jnp.zeros_like(lsum)
    rsum[...] = jnp.zeros_like(rsum)

    def stage_four(g):
        back = _dot(t_ref[2], window(g1, 8 * g, 384))
        part = jnp.zeros((C, 384), F32)
        skew = jnp.zeros((C, LN), F32)
        for r in range(8):
            kk = 8 * g + r
            value = back[r * C : (r + 1) * C] + bk[pl.ds((kk + 4) * C, C), :]
            value = value * d0[pl.ds((kk + M) * C, C), :]
            part = part + value
            wide = jnp.concatenate([value, jnp.zeros((C, 128), F32)], axis=1)
            skew = skew + (pltpu.roll(wide, r, 1) if r else wide)
        lsum[...] += part
        rsum[...] += pltpu.roll(skew, 8 * g, 1)

    def wgrad(layer):
        grads, fields, shift, near_at = ((g1, x0, 4, 12), (g2, x1, 8, 8))[layer]
        lhs = jnp.concatenate([grads[1, (8 * g + shift) * C : (8 * g + shift + 8) * C, :384] for g in range(4)], axis=1)
        for a in range(3):
            rhs = jnp.concatenate([fields[a, (8 * g + near_at) * C : (8 * g + near_at + 16) * C, :384] for g in range(4)], axis=1)
            acc[3 * layer + a] = _dot_nt(lhs, rhs)

    stages = ((stage_zero, 8), (stage_one, 7), (stage_two, 6), (stage_three, 5), (stage_four, 4))
    for stage, groups in stages:
        for g in range(groups):
            stage(g)
    wgrad(1)
    wgrad(0)

    rows = lax.broadcasted_iota(jnp.int32, (256, 512), 0) >> 5
    cols = lax.broadcasted_iota(jnp.int32, (256, 512), 1) >> 5
    delta = cols - rows - 4
    taps = []
    for layer in range(2):
        step = (s1, s2)[layer]
        for a in range(3):
            full = acc[3 * layer + a]
            for b in range(3):
                kept = jnp.where(delta == (b - 1) * step, full, 0.0)
                kept = jnp.sum(kept.reshape(8, C, 512), axis=0)
                kept = kept[:, :128] + kept[:, 128:256] + kept[:, 256:384] + kept[:, 384:]
                kept = kept + pltpu.roll(kept, 64, 1)
                taps.append(kept + pltpu.roll(kept, 32, 1))

    right = jnp.concatenate([rsum[...], jnp.zeros((C, 128), F32)], axis=1)
    right = pltpu.roll(right, first_diag, 1)
    both_ref[:C] = lsum[...]
    both_ref[C:] = right[:, :384]
    spill_ref[...] = right[:, 384:].astype(BF)
    both = jnp.concatenate(
        [jnp.concatenate([lsum[...], jnp.zeros((C, 256), F32)], axis=1), right], axis=0
    )
    none = jnp.zeros((2 * C, 640), BF)
    high, rest = _split(both)
    emb = jnp.concatenate([emb_ref[...], next_ref[4 * C + 48 :]], axis=1)
    part = _dot_nt(emb, jnp.concatenate([none, high], axis=0)) + _dot_nt(
        emb, jnp.concatenate([none, rest], axis=0)
    )
    for t in range(16):
        value = jnp.where(at < 32, taps[t], 0.0)
        if t < 2:
            value = jnp.where(at < 32, value, taps[16 + t])
        if t < 8:
            value = jnp.where(at < 64, value, part[C * t : C * t + C])
        sums_ref[C * t : C * t + C] = value


def pair_field(total_bins, total_diags, *operands):
    vmem = pl.BlockSpec(memory_space=pltpu.VMEM)
    return pl.pallas_call(
        functools.partial(pair_kernel, total_bins, total_diags),
        out_shape=(
            jax.ShapeDtypeStruct((32, 384), F32),
            jax.ShapeDtypeStruct((2 * C, 384), F32),
            jax.ShapeDtypeStruct((C, 256), BF),
            jax.ShapeDtypeStruct((512, 128), F32),
        ),
        in_specs=[pl.BlockSpec(memory_space=pltpu.SMEM)] * 2 + [vmem] * 7,
        out_specs=(vmem,) * 4,
        scratch_shapes=[
            pltpu.VMEM((3, 64 * C, LN), BF),
            pltpu.VMEM((3, 56 * C, LN), BF),
            pltpu.VMEM((3, 48 * C, LN), BF),
            pltpu.VMEM((3, 40 * C, LN), BF),
            pltpu.VMEM((64 * C, 384), F32),
            pltpu.VMEM((56 * C, LN), F32),
            pltpu.VMEM((40 * C, 384), F32),
            pltpu.VMEM((64, 8, LN), F32),
            pltpu.VMEM((C, 512), F32),
            pltpu.VMEM((C, 256), F32),
            pltpu.VMEM((C, LN), F32),
            pltpu.VMEM((48, LN), F32),
            pltpu.VMEM((6, 256, 512), F32),
            pltpu.VMEM((C, 384), F32),
            pltpu.VMEM((C, LN), F32),
        ],
        compiler_params=pltpu.CompilerParams(vmem_limit_bytes=56 * 2**20),
        cost_estimate=pl.CostEstimate(
            flops=12 * 10**9, bytes_accessed=5 * 10**6, transcendentals=3 * 10**6
        ),
        name="pair_field",
    )(*operands)


def on_device(
    embeddings, projection, dist_bias, conv_weight, head_weight, dilations, band_limit, cotangent
):
    bins = lax.axis_size("bin")
    diags = lax.axis_size("diag")
    diag_dev, rows_dev = cotangent.shape
    total_bins = rows_dev * bins
    total_diags = diag_dev * diags
    diag_at = lax.axis_index("diag")
    first_diag = diag_at * diag_dev

    pack, cots = prepare(total_bins, diags, embeddings, projection, cotangent, band_limit)
    bands = band_weights(dilations, conv_weight)
    got = lax.all_to_all(pack, "diag", 0, 0)
    got, bands = lax.optimization_barrier((got, bands))
    columns = projection.shape[1]
    features = diag_dev * diags
    emb_all = got[:, :diag_dev].reshape(features, rows_dev)
    flat = got[:, diag_dev + 8 :]
    proj_all = jnp.concatenate(
        [flat[:, :, columns * i : columns * (i + 1)] for i in range(4)], axis=1
    ).reshape(features, columns)
    edges = got[:, diag_dev : diag_dev + 8]
    before = lax.dynamic_index_in_dim(edges, jnp.maximum(diag_at - 1, 0), 0, False)
    after = lax.dynamic_index_in_dim(edges, jnp.minimum(diag_at + 1, diags - 1), 0, False)
    before = jnp.where(diag_at > 0, before.astype(F32), 0.0)
    after = jnp.where(diag_at < diags - 1, after.astype(F32), 0.0)
    projected = lax.dot_general(
        proj_all, emb_all, (((0,), (0,)), ((), ())), preferred_element_type=F32
    )
    own = jnp.concatenate([projected, before, cots, after], axis=0)

    up = [(i, i + 1) for i in range(bins - 1)]
    down = [(i + 1, i) for i in range(bins - 1)]
    high, rest = _split(projected)
    first = jnp.concatenate(
        [
            high[C:, :256],
            rest[C:, :256],
            jnp.concatenate([high[C:, 256:], rest[C:, 256:]], axis=1),
            jnp.concatenate([high[:C, :128], rest[:C, :128]], axis=1),
            own[2 * C :, :256].astype(BF),
            emb_all[:, :256],
        ],
        axis=0,
    )
    nxt = lax.ppermute(first, "bin", down)
    prv = lax.ppermute(own[:, rows_dev - 128 :], "bin", up)

    predicted, both, spill, sums = pair_field(
        total_bins, total_diags, dilations, head_weight, own, nxt, prv, dist_bias, band_limit,
        bands, emb_all,
    )

    spill = lax.ppermute(spill, "bin", up)
    shares = lax.all_to_all(sums.reshape(bins, 512 // bins, 128), "bin", 0, 0)
    both = both + jnp.pad(spill.astype(F32), ((C, 0), (0, rows_dev - spill.shape[1])))
    high, rest = _split(both)
    parts = _dot(
        jnp.concatenate([proj_all, proj_all], axis=1), jnp.concatenate([high, rest], axis=0)
    ).astype(BF).reshape(diags, diag_dev, rows_dev)
    share = jnp.sum(shares, axis=0)
    high, rest = _split(share)
    count = share.shape[0]
    tail = jnp.pad(jnp.concatenate([high, rest], axis=0), ((0, diag_dev - 2 * count), (0, 0)))
    parts = jnp.concatenate(
        [parts, jnp.broadcast_to(tail[None], (diags,) + tail.shape)], axis=2
    )
    total = jnp.sum(lax.all_to_all(parts, "diag", 0, 0).astype(F32), axis=0)
    grad_embed = total[:, :rows_dev]
    whole = total[:count, rows_dev:] + total[count : 2 * count, rows_dev:]
    every = lax.all_to_all(
        jnp.broadcast_to(whole[None], (bins,) + whole.shape), "bin", 0, 0
    ).reshape(bins * count, 128)
    scaling = 1.0 / math.sqrt(total_bins * total_diags)
    grad_conv = scaling * jnp.concatenate(
        [every[:, :C].reshape(16, C, C), every[: 2 * C, C : 2 * C].reshape(2, C, C)], axis=0
    ).reshape(2, 9, C, C)
    grad_proj = scaling * lax.dynamic_slice(
        every, (first_diag, 2 * C), (diag_dev, 2 * C)
    )
    return (predicted, grad_embed, grad_proj, grad_conv)


def solution(mesh):
    return jax.shard_map(
        on_device,
        mesh=mesh,
        in_specs=(
            P("diag", "bin"),
            P("diag", None),
            P(),
            P(),
            P(),
            P(),
            P("bin"),
            P("diag", "bin"),
        ),
        out_specs=(P("diag", "bin"), P("diag", "bin"), P("diag", None), P()),
        check_vma=False,
    )
```

```python
import functools
import math

import jax
import jax.numpy as jnp
from jax import lax
from jax.experimental import pallas as pl
from jax.experimental.pallas import tpu as pltpu
from jax.sharding import PartitionSpec as P

C = 32
M = 16
LN = 512
BF = jnp.bfloat16
F32 = jnp.float32


def _dot(a, b):
    return jnp.dot(a, b, preferred_element_type=F32)


def _dot_nt(a, b):
    return lax.dot_general(a, b, (((1,), (1,)), ((), ())), preferred_element_type=F32)


def _split(x):
    hi = x.astype(BF)
    return hi, (x - hi.astype(F32)).astype(BF)


def band_kernel(dil_ref, w_ref, t_ref):
    lane = lax.broadcasted_iota(jnp.int32, (C, 384), 1)
    spread = ((lane & 31) == lax.broadcasted_iota(jnp.int32, (C, 384), 0)).astype(F32).astype(BF)
    offset = (lane >> 5) - 4
    for layer in range(2):
        step = dil_ref[layer]
        for kind in range(2):
            for slot in range(3):
                wide = []
                for b in range(3):
                    if kind == 0:
                        wide.append(_dot(w_ref[layer, 3 * slot + b], spread))
                    else:
                        w = w_ref[layer, 3 * (2 - slot) + 2 - b]
                        wide.append(
                            lax.dot_general(
                                w, spread, (((0,), (0,)), ((), ())), preferred_element_type=F32
                            )
                        )
                for j in range(4):
                    value = jnp.zeros((C, 384), F32)
                    for b in range(3):
                        value = jnp.where(offset == j + (b - 1) * step, wide[b], value)
                    t_ref[2 * kind + layer, C * j : C * j + C, 384 * slot : 384 * slot + 384] = (
                        value.astype(BF)
                    )


def band_weights(dilations, conv_weight):
    vmem = pl.BlockSpec(memory_space=pltpu.VMEM)
    return pl.pallas_call(
        band_kernel,
        out_shape=jax.ShapeDtypeStruct((4, 128, 1152), BF),
        in_specs=[pl.BlockSpec(memory_space=pltpu.SMEM), vmem],
        out_specs=vmem,
        compiler_params=pltpu.CompilerParams(vmem_limit_bytes=16 * 2**20),
        cost_estimate=pl.CostEstimate(flops=10**8, bytes_accessed=2 * 10**6, transcendentals=0),
        name="band_weights",
    )(dilations, conv_weight)


def prepare_kernel(
    total_bins, emb_hbm, proj_hbm, cot_hbm, limit_hbm, pack_ref, cots_ref,
    emb_ref, proj_ref, cot_ref, limit_ref, sems,
):
    copies = [
        pltpu.make_async_copy(source, target, sems.at[i])
        for i, (source, target) in enumerate(
            ((emb_hbm, emb_ref), (proj_hbm, proj_ref), (cot_hbm, cot_ref), (limit_hbm, limit_ref))
        )
    ]
    for copy in copies:
        copy.start()
    for copy in copies:
        copy.wait()
    diag_dev, rows_dev = cot_ref.shape
    diag_at = lax.axis_index("diag")
    first_row = lax.axis_index("bin") * rows_dev
    shape = (diag_dev, rows_dev)
    bin_id = first_row + lax.broadcasted_iota(jnp.int32, shape, 1)
    diag_id = diag_at * diag_dev + lax.broadcasted_iota(jnp.int32, shape, 0)
    counted = (bin_id + diag_id < total_bins) & (diag_id < limit_ref[...][None, :])
    cots = jnp.where(counted, cot_ref[...], 0.0)
    cots_ref[...] = cots
    columns = proj_ref.shape[1]
    quarter = diag_dev // 4
    proj = proj_ref[...].astype(F32)
    flat = jnp.concatenate(
        [proj[quarter * i : quarter * (i + 1)] for i in range(4)]
        + [jnp.zeros((quarter, rows_dev - 4 * columns), F32)],
        axis=1,
    )
    last = jnp.concatenate([cots[diag_dev - 8 :], flat], axis=0)
    first = jnp.concatenate([cots[:8], flat], axis=0)
    for peer in range(pack_ref.shape[0]):
        pack_ref[peer, :diag_dev] = emb_ref[...]
        pack_ref[peer, diag_dev:] = jnp.where(peer > diag_at, last, first).astype(BF)


def prepare(total_bins, diags, *operands):
    diag_dev, rows_dev = operands[0].shape
    vmem = pl.BlockSpec(memory_space=pltpu.VMEM)
    return pl.pallas_call(
        functools.partial(prepare_kernel, total_bins),
        out_shape=(
            jax.ShapeDtypeStruct((diags, diag_dev + 16, rows_dev), BF),
            jax.ShapeDtypeStruct((diag_dev, rows_dev), F32),
        ),
        in_specs=[pl.BlockSpec(memory_space=pl.ANY)] * 4,
        out_specs=(vmem, vmem),
        scratch_shapes=[pltpu.VMEM(x.shape, x.dtype) for x in operands]
        + [pltpu.SemaphoreType.DMA((4,))],
        compiler_params=pltpu.CompilerParams(vmem_limit_bytes=56 * 2**20),
        name="prepare",
    )(*operands)


def pair_kernel(
    total_bins, total_diags,
    dil_ref, head_ref, next_hbm, prev_hbm, own_ref, bias_ref, limit_ref, t_ref, emb_ref,
    pred_ref, both_ref, spill_ref, sums_ref,
    x0, x1, g2, g1, d0, d1, bk, mk, vbuf, ubuf, left, gwide, acc, lsum, rsum, next_ref, prev_ref, sems,
):
    arrivals = [
        pltpu.make_async_copy(next_hbm, next_ref, sems.at[0]),
        pltpu.make_async_copy(prev_hbm, prev_ref, sems.at[1]),
    ]
    for copy in arrivals:
        copy.start()
    first_row = lax.axis_index("bin") * 384
    first_diag = lax.axis_index("diag") * 32
    s1 = dil_ref[0]
    s2 = dil_ref[1]

    lane = lax.broadcasted_iota(jnp.int32, (8, LN), 1)
    low = lax.broadcasted_iota(jnp.int32, (C, 128), 1) < 64
    bin_id = first_row + jnp.where(lane < 448, lane, lane - LN)
    bin_ok = (bin_id >= 0) & (bin_id < total_bins)

    own = own_ref[...]
    for copy in arrivals:
        copy.wait()
    prv = prev_ref[...]

    def rows_of(first, count, lanes):
        return next_ref[first : first + count, lanes].astype(F32)

    every, head_half, tail_half = slice(None), slice(0, 128), slice(128, 256)
    next_right = jnp.concatenate(
        [
            rows_of(0, C, every) + rows_of(C, C, every),
            rows_of(2 * C, C, head_half) + rows_of(2 * C, C, tail_half),
        ],
        axis=1,
    )
    next_left = rows_of(3 * C, C, head_half) + rows_of(3 * C, C, tail_half)
    next_cots = rows_of(4 * C, 48, head_half)
    left[:, :384] = own[:C]
    left[:, 384:] = jnp.where(low, next_left, prv[:C])
    low48 = lax.broadcasted_iota(jnp.int32, (48, 128), 1) < 64
    gwide[:, :384] = own[2 * C :]
    gwide[:, 384:] = jnp.where(low48, next_cots, prv[2 * C :])
    line = jnp.concatenate([prv[C : 2 * C], own[C : 2 * C], next_right], axis=1)
    bias = pltpu.roll(bias_ref[...], lax.rem(256 + M - first_diag, 256), 1)
    vbuf[...] = pltpu.roll(line, 784 - first_diag, 1)[:, :512]
    ubuf[...] = pltpu.roll(line, lax.rem(912 - first_diag, 896), 1)[:, :256]

    at = lax.broadcasted_iota(jnp.int32, (C, 128), 1)

    def spread(ref, rows, shift):
        for row in rows:
            cols = [ref[1, row : row + C, 128 * i : 128 * i + 128] for i in range(4)]
            later = [pltpu.roll(v, shift, 1) for v in cols]
            sooner = [pltpu.roll(v, 128 - shift, 1) for v in cols]
            for i in range(4):
                here = slice(128 * i, 128 * i + 128)
                ref[0, row : row + C, here] = jnp.where(at < shift, later[i - 1], later[i])
                ref[2, row : row + C, here] = jnp.where(
                    at < 128 - shift, sooner[i], sooner[(i + 1) % 4]
                )

    def times(value, mask):
        return (value.reshape(4, 8, value.shape[1]) * mask[None]).reshape(value.shape)

    def stage_zero(g, back):
        for r in range(8):
            k = 8 * g + r
            diag_id = first_diag - M + k
            ok = bin_ok & (bin_id + diag_id < total_bins) & (diag_id >= 0) & (diag_id < total_diags)
            mask = ok.astype(F32)
            mk[k] = mask
            by = (128 - k) % 128
            v = [pltpu.roll(vbuf[:, 128 * i : 128 * i + 128], by, 1) for i in range(4)]
            u = [pltpu.roll(ubuf[:, 128 * i : 128 * i + 128], by, 1) for i in range(2)]
            here = at < 128 - k
            shifted = jnp.concatenate(
                [jnp.where(here, v[i], v[i + 1]) for i in range(3)]
                + [jnp.where(low, v[3], jnp.where(here, u[0], u[1]))],
                axis=1,
            )
            t = jnp.tanh(left[...] + shifted + bias[:, k : k + 1])
            row = k * C
            x0[1, row : row + C] = times(t, mask).astype(BF)
            d0[pl.ds(row, C), :] = times(1.0 - t[:, :384] * t[:, :384], mask[:, :384])
        spread(x0, range(8 * g * C, (8 * g + 8) * C, C), s1)


    def window(ref, first, width):
        return [ref[a, first * C : (first + 12) * C, :width] for a in range(3)]

    def conv(kind, ref, first, width):
        return jnp.concatenate(
            [
                _dot(t_ref[kind], jnp.concatenate(window(ref, at_offset, width), axis=0))
                for at_offset in (first, first + 4)
            ],
            axis=0,
        )

    def stage_one(g, back):
        t1 = jnp.tanh(back)
        for r in range(8):
            k = 4 + 8 * g + r
            mask = mk[k]
            t = t1[r * C : (r + 1) * C]
            base = x0[1, pl.ds(k * C, C), :].astype(F32)
            x1[1, pl.ds((k - 4) * C, C), :] = times(base + t, mask).astype(BF)
            d1[pl.ds((k - 4) * C, C), :] = times(1.0 - t * t, mask)
        spread(x1, range(8 * g * C, (8 * g + 8) * C, C), s2)


    head = jnp.concatenate([jnp.full((1, LN), head_ref[c], F32) for c in range(C)], axis=0)
    limits = limit_ref[...][None, :]
    own_bin = first_row + lax.broadcasted_iota(jnp.int32, (8, 384), 1)
    own_row = lax.broadcasted_iota(jnp.int32, (8, 384), 0)

    def stage_two(g, back):
        t2 = jnp.tanh(back)
        cots = gwide[pl.ds(8 * g, 8), :]
        lines = []
        for r in range(8):
            k = 8 + 8 * g + r
            t = t2[r * C : (r + 1) * C]
            value = cots[r : r + 1] * (head * (1.0 - t * t))
            g2[1, pl.ds((k - 8) * C, C), :] = value.astype(BF)
            lines.append(jnp.sum(head[:, :384] * t[:, :384], axis=0, keepdims=True))
        spread(g2, range(8 * g * C, (8 * g + 8) * C, C), s2)

        if 1 <= g < 5:
            diag_id = first_diag + 8 * (g - 1) + own_row
            ok = (own_bin + diag_id < total_bins) & (diag_id < limits)
            pred_ref[pl.ds(8 * (g - 1), 8), :] = jnp.where(
                ok, jnp.concatenate(lines, axis=0), 0.0
            )


    def stage_three(g, back):
        for r in range(8):
            k = 12 + 8 * g + r
            value = back[r * C : (r + 1) * C]
            at = (k - 12) * C
            g1[1, pl.ds(at, C), :] = (value * d1[pl.ds((k - 4) * C, C), :]).astype(BF)
            bk[pl.ds(at, C), :] = times(value, mk[k])[:, :384]
        spread(g1, range(8 * g * C, (8 * g + 8) * C, C), s1)


    lsum[...] = jnp.zeros_like(lsum)
    rsum[...] = jnp.zeros_like(rsum)

    def stage_four(g, back):
        part = jnp.zeros((C, 384), F32)
        skew = jnp.zeros((C, LN), F32)
        for r in range(8):
            kk = 8 * g + r
            value = back[r * C : (r + 1) * C] + bk[pl.ds((kk + 4) * C, C), :]
            value = value * d0[pl.ds((kk + M) * C, C), :]
            part = part + value
            wide = jnp.concatenate([value, jnp.zeros((C, 128), F32)], axis=1)
            skew = skew + (pltpu.roll(wide, r, 1) if r else wide)
        lsum[...] += part
        rsum[...] += pltpu.roll(skew, 8 * g, 1)

    def wgrad(layer):
        grads, fields, shift, near_at = ((g1, x0, 4, 12), (g2, x1, 8, 8))[layer]
        lhs = jnp.concatenate([grads[1, (8 * g + shift) * C : (8 * g + shift + 8) * C, :384] for g in range(4)], axis=1)
        for a in range(3):
            rhs = jnp.concatenate([fields[a, (8 * g + near_at) * C : (8 * g + near_at + 16) * C, :384] for g in range(4)], axis=1)
            acc[3 * layer + a] = _dot_nt(lhs, rhs)

    stages = (
        (stage_zero, 8, None),
        (stage_one, 7, lambda g: conv(0, x0, 8 * g, LN)),
        (stage_two, 6, lambda g: conv(1, x1, 8 * g, LN)),
        (stage_three, 5, lambda g: conv(3, g2, 8 * g, LN)),
        (stage_four, 4, lambda g: conv(2, g1, 8 * g, 384)),
    )
    for stage, groups, dot in stages:
        for g in range(groups):
            stage(g, dot(g) if dot else None)
    wgrad(1)
    wgrad(0)
    rows = lax.broadcasted_iota(jnp.int32, (256, 512), 0) >> 5
    cols = lax.broadcasted_iota(jnp.int32, (256, 512), 1) >> 5
    delta = cols - rows - 4
    taps = []
    for layer in range(2):
        step = (s1, s2)[layer]
        for a in range(3):
            full = acc[3 * layer + a]
            for b in range(3):
                kept = jnp.where(delta == (b - 1) * step, full, 0.0)
                kept = jnp.sum(kept.reshape(8, C, 512), axis=0)
                kept = kept[:, :128] + kept[:, 128:256] + kept[:, 256:384] + kept[:, 384:]
                kept = kept + pltpu.roll(kept, 64, 1)
                taps.append(kept + pltpu.roll(kept, 32, 1))


    right = jnp.concatenate([rsum[...], jnp.zeros((C, 128), F32)], axis=1)
    right = pltpu.roll(right, first_diag, 1)
    both_ref[:C] = lsum[...]
    both_ref[C:] = right[:, :384]
    spill_ref[...] = right[:, 384:].astype(BF)
    both = jnp.concatenate(
        [jnp.concatenate([lsum[...], jnp.zeros((C, 256), F32)], axis=1), right], axis=0
    )
    none = jnp.zeros((2 * C, 640), BF)
    high, rest = _split(both)
    emb = jnp.concatenate([emb_ref[...], next_ref[4 * C + 48 :]], axis=1)
    part = _dot_nt(emb, jnp.concatenate([none, high], axis=0)) + _dot_nt(
        emb, jnp.concatenate([none, rest], axis=0)
    )
    for t in range(16):
        value = jnp.where(at < 32, taps[t], 0.0)
        if t < 2:
            value = jnp.where(at < 32, value, taps[16 + t])
        if t < 8:
            value = jnp.where(at < 64, value, part[C * t : C * t + C])
        sums_ref[C * t : C * t + C] = value


def pair_field(total_bins, total_diags, *operands):
    vmem = pl.BlockSpec(memory_space=pltpu.VMEM)
    return pl.pallas_call(
        functools.partial(pair_kernel, total_bins, total_diags),
        out_shape=(
            jax.ShapeDtypeStruct((32, 384), F32),
            jax.ShapeDtypeStruct((2 * C, 384), F32),
            jax.ShapeDtypeStruct((C, 256), BF),
            jax.ShapeDtypeStruct((512, 128), F32),
        ),
        in_specs=[pl.BlockSpec(memory_space=pltpu.SMEM)] * 2
        + [pl.BlockSpec(memory_space=pl.ANY)] * 2
        + [vmem] * 5,
        out_specs=(vmem,) * 4,
        scratch_shapes=[
            pltpu.VMEM((3, 64 * C, LN), BF),
            pltpu.VMEM((3, 56 * C, LN), BF),
            pltpu.VMEM((3, 48 * C, LN), BF),
            pltpu.VMEM((3, 40 * C, LN), BF),
            pltpu.VMEM((64 * C, 384), F32),
            pltpu.VMEM((56 * C, LN), F32),
            pltpu.VMEM((40 * C, 384), F32),
            pltpu.VMEM((64, 8, LN), F32),
            pltpu.VMEM((C, 512), F32),
            pltpu.VMEM((C, 256), F32),
            pltpu.VMEM((C, LN), F32),
            pltpu.VMEM((48, LN), F32),
            pltpu.VMEM((6, 256, 512), F32),
            pltpu.VMEM((C, 384), F32),
            pltpu.VMEM((C, LN), F32),
            pltpu.VMEM((432, 256), BF),
            pltpu.VMEM((112, 128), F32),
            pltpu.SemaphoreType.DMA((2,)),
        ],
        compiler_params=pltpu.CompilerParams(vmem_limit_bytes=56 * 2**20),
        cost_estimate=pl.CostEstimate(
            flops=12 * 10**9, bytes_accessed=5 * 10**6, transcendentals=3 * 10**6
        ),
        name="pair_field",
    )(*operands)


def finish_kernel(scaling, every_ref, proj_ref, conv_ref):
    first_diag = pl.multiple_of(lax.axis_index("diag") * C, C)
    proj_ref[...] = scaling * every_ref[pl.ds(first_diag, C), 2 * C :]
    for tap in range(18):
        if tap < 16:
            value = every_ref[C * tap : C * tap + C, :C]
        else:
            value = every_ref[C * (tap - 16) : C * (tap - 15), C : 2 * C]
        conv_ref[tap // 9, tap % 9] = scaling * value


def finish(scaling, every):
    vmem = pl.BlockSpec(memory_space=pltpu.VMEM)
    return pl.pallas_call(
        functools.partial(finish_kernel, scaling),
        out_shape=(
            jax.ShapeDtypeStruct((C, 2 * C), F32),
            jax.ShapeDtypeStruct((2, 9, C, C), F32),
        ),
        in_specs=[vmem],
        out_specs=(vmem, vmem),
        compiler_params=pltpu.CompilerParams(vmem_limit_bytes=16 * 2**20),
        name="finish",
    )(every)


def on_device(
    embeddings, projection, dist_bias, conv_weight, head_weight, dilations, band_limit, cotangent
):
    bins = lax.axis_size("bin")
    diags = lax.axis_size("diag")
    diag_dev, rows_dev = cotangent.shape
    total_bins = rows_dev * bins
    total_diags = diag_dev * diags
    diag_at = lax.axis_index("diag")
    first_diag = diag_at * diag_dev

    pack, cots = prepare(total_bins, diags, embeddings, projection, cotangent, band_limit)
    bands = band_weights(dilations, conv_weight)
    got = lax.all_to_all(pack, "diag", 0, 0)
    got, bands = lax.optimization_barrier((got, bands))
    columns = projection.shape[1]
    features = diag_dev * diags
    emb_all = got[:, :diag_dev].reshape(features, rows_dev)
    flat = got[:, diag_dev + 8 :]
    proj_all = jnp.concatenate(
        [flat[:, :, columns * i : columns * (i + 1)] for i in range(4)], axis=1
    ).reshape(features, columns)
    edges = got[:, diag_dev : diag_dev + 8]
    before = lax.dynamic_index_in_dim(edges, jnp.maximum(diag_at - 1, 0), 0, False)
    after = lax.dynamic_index_in_dim(edges, jnp.minimum(diag_at + 1, diags - 1), 0, False)
    before = jnp.where(diag_at > 0, before.astype(F32), 0.0)
    after = jnp.where(diag_at < diags - 1, after.astype(F32), 0.0)
    projected = lax.dot_general(
        proj_all, emb_all, (((0,), (0,)), ((), ())), preferred_element_type=F32
    )
    own = jnp.concatenate([projected, before, cots, after], axis=0)

    up = [(i, i + 1) for i in range(bins - 1)]
    down = [(i + 1, i) for i in range(bins - 1)]
    high, rest = _split(projected)
    first = jnp.concatenate(
        [
            high[C:, :256],
            rest[C:, :256],
            jnp.concatenate([high[C:, 256:], rest[C:, 256:]], axis=1),
            jnp.concatenate([high[:C, :128], rest[:C, :128]], axis=1),
            own[2 * C :, :256].astype(BF),
            emb_all[:, :256],
        ],
        axis=0,
    )
    nxt = lax.ppermute(first, "bin", down)
    prv = lax.ppermute(own[:, rows_dev - 128 :], "bin", up)

    predicted, both, spill, sums = pair_field(
        total_bins, total_diags, dilations, head_weight, nxt, prv, own, dist_bias, band_limit,
        bands, emb_all,
    )

    spill = lax.ppermute(spill, "bin", up)
    shares = lax.all_to_all(sums.reshape(bins, 512 // bins, 128), "bin", 0, 0)
    both = both + jnp.pad(spill.astype(F32), ((C, 0), (0, rows_dev - spill.shape[1])))
    high, rest = _split(both)
    parts = _dot(
        jnp.concatenate([proj_all, proj_all], axis=1), jnp.concatenate([high, rest], axis=0)
    ).astype(BF).reshape(diags, diag_dev, rows_dev)
    share = jnp.sum(shares, axis=0)
    high, rest = _split(share)
    count = share.shape[0]
    tail = jnp.pad(jnp.concatenate([high, rest], axis=0), ((0, diag_dev - 2 * count), (0, 0)))
    parts = jnp.concatenate(
        [parts, jnp.broadcast_to(tail[None], (diags,) + tail.shape)], axis=2
    )
    total = jnp.sum(lax.all_to_all(parts, "diag", 0, 0).astype(F32), axis=0)
    grad_embed = total[:, :rows_dev]
    whole = total[:count, rows_dev:] + total[count : 2 * count, rows_dev:]
    every = lax.all_to_all(
        jnp.broadcast_to(whole[None], (bins,) + whole.shape), "bin", 0, 0
    ).reshape(bins * count, 128)
    scaling = 1.0 / math.sqrt(total_bins * total_diags)
    grad_proj, grad_conv = finish(scaling, every)
    return (predicted, grad_embed, grad_proj, grad_conv)


def solution(mesh):
    return jax.shard_map(
        on_device,
        mesh=mesh,
        in_specs=(
            P("diag", "bin"),
            P("diag", None),
            P(),
            P(),
            P(),
            P(),
            P("bin"),
            P("diag", "bin"),
        ),
        out_specs=(P("diag", "bin"), P("diag", "bin"), P("diag", None), P()),
        check_vma=False,
    )
```

```python
import functools
import math

import jax
import jax.numpy as jnp
from jax import lax
from jax.experimental import pallas as pl
from jax.experimental.pallas import tpu as pltpu
from jax.sharding import PartitionSpec as P

C = 32
M = 16
LN = 512
BF = jnp.bfloat16
F32 = jnp.float32


def _dot(a, b):
    return jnp.dot(a, b, preferred_element_type=F32)


def _dot_nt(a, b):
    return lax.dot_general(a, b, (((1,), (1,)), ((), ())), preferred_element_type=F32)


def _split(x):
    hi = x.astype(BF)
    return hi, (x - hi.astype(F32)).astype(BF)


def band_kernel(dil_ref, w_ref, t_ref):
    lane = lax.broadcasted_iota(jnp.int32, (C, 384), 1)
    spread = ((lane & 31) == lax.broadcasted_iota(jnp.int32, (C, 384), 0)).astype(F32).astype(BF)
    offset = (lane >> 5) - 4
    for layer in range(2):
        step = dil_ref[layer]
        for kind in range(2):
            for slot in range(3):
                wide = []
                for b in range(3):
                    if kind == 0:
                        wide.append(_dot(w_ref[layer, 3 * slot + b], spread))
                    else:
                        w = w_ref[layer, 3 * (2 - slot) + 2 - b]
                        wide.append(
                            lax.dot_general(
                                w, spread, (((0,), (0,)), ((), ())), preferred_element_type=F32
                            )
                        )
                for j in range(4):
                    value = jnp.zeros((C, 384), F32)
                    for b in range(3):
                        value = jnp.where(offset == j + (b - 1) * step, wide[b], value)
                    t_ref[2 * kind + layer, C * j : C * j + C, 384 * slot : 384 * slot + 384] = (
                        value.astype(BF)
                    )


def band_weights(dilations, conv_weight):
    vmem = pl.BlockSpec(memory_space=pltpu.VMEM)
    return pl.pallas_call(
        band_kernel,
        out_shape=jax.ShapeDtypeStruct((4, 128, 1152), BF),
        in_specs=[pl.BlockSpec(memory_space=pltpu.SMEM), vmem],
        out_specs=vmem,
        compiler_params=pltpu.CompilerParams(vmem_limit_bytes=16 * 2**20),
        cost_estimate=pl.CostEstimate(flops=10**8, bytes_accessed=2 * 10**6, transcendentals=0),
        name="band_weights",
    )(dilations, conv_weight)


def prepare_kernel(
    total_bins, emb_hbm, proj_hbm, cot_hbm, limit_hbm, pack_ref, cots_ref,
    emb_ref, proj_ref, cot_ref, limit_ref, sems,
):
    copies = [
        pltpu.make_async_copy(source, target, sems.at[i])
        for i, (source, target) in enumerate(
            ((emb_hbm, emb_ref), (proj_hbm, proj_ref), (cot_hbm, cot_ref), (limit_hbm, limit_ref))
        )
    ]
    for copy in copies:
        copy.start()
    for copy in copies:
        copy.wait()
    diag_dev, rows_dev = cot_ref.shape
    diag_at = lax.axis_index("diag")
    first_row = lax.axis_index("bin") * rows_dev
    shape = (diag_dev, rows_dev)
    bin_id = first_row + lax.broadcasted_iota(jnp.int32, shape, 1)
    diag_id = diag_at * diag_dev + lax.broadcasted_iota(jnp.int32, shape, 0)
    counted = (bin_id + diag_id < total_bins) & (diag_id < limit_ref[...][None, :])
    cots = jnp.where(counted, cot_ref[...], 0.0)
    cots_ref[...] = cots
    columns = proj_ref.shape[1]
    quarter = diag_dev // 4
    proj = proj_ref[...].astype(F32)
    flat = jnp.concatenate(
        [proj[quarter * i : quarter * (i + 1)] for i in range(4)]
        + [jnp.zeros((quarter, rows_dev - 4 * columns), F32)],
        axis=1,
    )
    last = jnp.concatenate([cots[diag_dev - 8 :], flat], axis=0)
    first = jnp.concatenate([cots[:8], flat], axis=0)
    for peer in range(pack_ref.shape[0]):
        pack_ref[peer, :diag_dev] = emb_ref[...]
        pack_ref[peer, diag_dev:] = jnp.where(peer > diag_at, last, first).astype(BF)


def prepare(total_bins, diags, *operands):
    diag_dev, rows_dev = operands[0].shape
    vmem = pl.BlockSpec(memory_space=pltpu.VMEM)
    return pl.pallas_call(
        functools.partial(prepare_kernel, total_bins),
        out_shape=(
            jax.ShapeDtypeStruct((diags, diag_dev + 16, rows_dev), BF),
            jax.ShapeDtypeStruct((diag_dev, rows_dev), F32),
        ),
        in_specs=[pl.BlockSpec(memory_space=pltpu.HBM)] * 4,
        out_specs=(vmem, vmem),
        scratch_shapes=[pltpu.VMEM(x.shape, x.dtype) for x in operands]
        + [pltpu.SemaphoreType.DMA((4,))],
        compiler_params=pltpu.CompilerParams(vmem_limit_bytes=16 * 2**20),
        name="prepare",
    )(*operands)


def pair_kernel(
    total_bins, total_diags,
    dil_ref, head_ref, next_ref, prev_ref, own_ref, bias_ref, limit_ref, t_ref, emb_ref,
    pred_ref, both_ref, spill_ref, sums_ref,
    x0, x1, g2, g1, d0, d1, bk, mk, vbuf, ubuf, left, gwide, acc, lsum, rsum,
):
    first_row = lax.axis_index("bin") * 384
    first_diag = lax.axis_index("diag") * 32
    s1 = dil_ref[0]
    s2 = dil_ref[1]

    lane = lax.broadcasted_iota(jnp.int32, (8, LN), 1)
    low = lax.broadcasted_iota(jnp.int32, (C, 128), 1) < 64
    bin_id = first_row + jnp.where(lane < 448, lane, lane - LN)
    bin_ok = (bin_id >= 0) & (bin_id < total_bins)

    own = own_ref[...]
    prv = prev_ref[...]

    def rows_of(first, count, lanes):
        return next_ref[first : first + count, lanes].astype(F32)

    every, head_half, tail_half = slice(None), slice(0, 128), slice(128, 256)
    next_right = jnp.concatenate(
        [
            rows_of(0, C, every) + rows_of(C, C, every),
            rows_of(2 * C, C, head_half) + rows_of(2 * C, C, tail_half),
        ],
        axis=1,
    )
    next_left = rows_of(3 * C, C, head_half) + rows_of(3 * C, C, tail_half)
    next_cots = rows_of(4 * C, 48, head_half)
    left[:, :384] = own[:C]
    left[:, 384:] = jnp.where(low, next_left, prv[:C])
    low48 = lax.broadcasted_iota(jnp.int32, (48, 128), 1) < 64
    gwide[:, :384] = own[2 * C :]
    gwide[:, 384:] = jnp.where(low48, next_cots, prv[2 * C :])
    line = jnp.concatenate([prv[C : 2 * C], own[C : 2 * C], next_right], axis=1)
    bias = pltpu.roll(bias_ref[...], lax.rem(256 + M - first_diag, 256), 1)
    vbuf[...] = pltpu.roll(line, 784 - first_diag, 1)[:, :512]
    ubuf[...] = pltpu.roll(line, lax.rem(912 - first_diag, 896), 1)[:, :256]

    at = lax.broadcasted_iota(jnp.int32, (C, 128), 1)

    def spread(ref, rows, shift):
        for row in rows:
            cols = [ref[1, row : row + C, 128 * i : 128 * i + 128] for i in range(4)]
            later = [pltpu.roll(v, shift, 1) for v in cols]
            sooner = [pltpu.roll(v, 128 - shift, 1) for v in cols]
            for i in range(4):
                here = slice(128 * i, 128 * i + 128)
                ref[0, row : row + C, here] = jnp.where(at < shift, later[i - 1], later[i])
                ref[2, row : row + C, here] = jnp.where(
                    at < 128 - shift, sooner[i], sooner[(i + 1) % 4]
                )

    def times(value, mask):
        return (value.reshape(4, 8, value.shape[1]) * mask[None]).reshape(value.shape)

    def stage_zero(g, back):
        for r in range(8):
            k = 8 * g + r
            diag_id = first_diag - M + k
            ok = bin_ok & (bin_id + diag_id < total_bins) & (diag_id >= 0) & (diag_id < total_diags)
            mask = ok.astype(F32)
            mk[k] = mask
            by = (128 - k) % 128
            v = [pltpu.roll(vbuf[:, 128 * i : 128 * i + 128], by, 1) for i in range(4)]
            u = [pltpu.roll(ubuf[:, 128 * i : 128 * i + 128], by, 1) for i in range(2)]
            here = at < 128 - k
            shifted = jnp.concatenate(
                [jnp.where(here, v[i], v[i + 1]) for i in range(3)]
                + [jnp.where(low, v[3], jnp.where(here, u[0], u[1]))],
                axis=1,
            )
            t = jnp.tanh(left[...] + shifted + bias[:, k : k + 1])
            row = k * C
            x0[1, row : row + C] = times(t, mask).astype(BF)
            d0[pl.ds(row, C), :] = times(1.0 - t[:, :384] * t[:, :384], mask[:, :384])
        spread(x0, range(8 * g * C, (8 * g + 8) * C, C), s1)


    def window(ref, first, width):
        return [ref[a, first * C : (first + 12) * C, :width] for a in range(3)]

    def conv(kind, ref, first, width):
        return jnp.concatenate(
            [
                _dot(t_ref[kind], jnp.concatenate(window(ref, at_offset, width), axis=0))
                for at_offset in (first, first + 4)
            ],
            axis=0,
        )

    def stage_one(g, back):
        t1 = jnp.tanh(back)
        for r in range(8):
            k = 4 + 8 * g + r
            mask = mk[k]
            t = t1[r * C : (r + 1) * C]
            base = x0[1, pl.ds(k * C, C), :].astype(F32)
            x1[1, pl.ds((k - 4) * C, C), :] = times(base + t, mask).astype(BF)
            d1[pl.ds((k - 4) * C, C), :] = times(1.0 - t * t, mask)
        spread(x1, range(8 * g * C, (8 * g + 8) * C, C), s2)


    head = jnp.concatenate([jnp.full((1, LN), head_ref[c], F32) for c in range(C)], axis=0)
    limits = limit_ref[...][None, :]
    own_bin = first_row + lax.broadcasted_iota(jnp.int32, (8, 384), 1)
    own_row = lax.broadcasted_iota(jnp.int32, (8, 384), 0)

    def stage_two(g, back):
        t2 = jnp.tanh(back)
        cots = gwide[pl.ds(8 * g, 8), :]
        lines = []
        for r in range(8):
            k = 8 + 8 * g + r
            t = t2[r * C : (r + 1) * C]
            value = cots[r : r + 1] * (head * (1.0 - t * t))
            g2[1, pl.ds((k - 8) * C, C), :] = value.astype(BF)
            lines.append(jnp.sum(head[:, :384] * t[:, :384], axis=0, keepdims=True))
        spread(g2, range(8 * g * C, (8 * g + 8) * C, C), s2)

        if 1 <= g < 5:
            diag_id = first_diag + 8 * (g - 1) + own_row
            ok = (own_bin + diag_id < total_bins) & (diag_id < limits)
            pred_ref[pl.ds(8 * (g - 1), 8), :] = jnp.where(
                ok, jnp.concatenate(lines, axis=0), 0.0
            )


    def stage_three(g, back):
        for r in range(8):
            k = 12 + 8 * g + r
            value = back[r * C : (r + 1) * C]
            at = (k - 12) * C
            g1[1, pl.ds(at, C), :] = (value * d1[pl.ds((k - 4) * C, C), :]).astype(BF)
            bk[pl.ds(at, C), :] = times(value, mk[k])[:, :384]
        spread(g1, range(8 * g * C, (8 * g + 8) * C, C), s1)


    lsum[...] = jnp.zeros_like(lsum)
    rsum[...] = jnp.zeros_like(rsum)

    def stage_four(g, back):
        part = jnp.zeros((C, 384), F32)
        skew = jnp.zeros((C, LN), F32)
        for r in range(8):
            kk = 8 * g + r
            value = back[r * C : (r + 1) * C] + bk[pl.ds((kk + 4) * C, C), :]
            value = value * d0[pl.ds((kk + M) * C, C), :]
            part = part + value
            wide = jnp.concatenate([value, jnp.zeros((C, 128), F32)], axis=1)
            skew = skew + (pltpu.roll(wide, r, 1) if r else wide)
        lsum[...] += part
        rsum[...] += pltpu.roll(skew, 8 * g, 1)

    def wgrad(layer):
        grads, fields, shift, near_at = ((g1, x0, 4, 12), (g2, x1, 8, 8))[layer]
        lhs = jnp.concatenate([grads[1, (8 * g + shift) * C : (8 * g + shift + 8) * C, :384] for g in range(4)], axis=1)
        for a in range(3):
            rhs = jnp.concatenate([fields[a, (8 * g + near_at) * C : (8 * g + near_at + 16) * C, :384] for g in range(4)], axis=1)
            acc[3 * layer + a] = _dot_nt(lhs, rhs)

    stages = (
        (stage_zero, 8, None),
        (stage_one, 7, lambda g: conv(0, x0, 8 * g, LN)),
        (stage_two, 6, lambda g: conv(1, x1, 8 * g, LN)),
        (stage_three, 5, lambda g: conv(3, g2, 8 * g, LN)),
        (stage_four, 4, lambda g: conv(2, g1, 8 * g, 384)),
    )
    for stage, groups, dot in stages:
        for g in range(groups):
            stage(g, dot(g) if dot else None)
    wgrad(1)
    wgrad(0)
    rows = lax.broadcasted_iota(jnp.int32, (256, 512), 0) >> 5
    cols = lax.broadcasted_iota(jnp.int32, (256, 512), 1) >> 5
    delta = cols - rows - 4
    taps = []
    for layer in range(2):
        step = (s1, s2)[layer]
        for a in range(3):
            full = acc[3 * layer + a]
            for b in range(3):
                kept = jnp.where(delta == (b - 1) * step, full, 0.0)
                kept = jnp.sum(kept.reshape(8, C, 512), axis=0)
                kept = kept[:, :128] + kept[:, 128:256] + kept[:, 256:384] + kept[:, 384:]
                kept = kept + pltpu.roll(kept, 64, 1)
                taps.append(kept + pltpu.roll(kept, 32, 1))


    right = jnp.concatenate([rsum[...], jnp.zeros((C, 128), F32)], axis=1)
    right = pltpu.roll(right, first_diag, 1)
    both_ref[:C] = lsum[...]
    both_ref[C:] = right[:, :384]
    spill_ref[...] = right[:, 384:].astype(BF)
    both = jnp.concatenate(
        [jnp.concatenate([lsum[...], jnp.zeros((C, 256), F32)], axis=1), right], axis=0
    )
    none = jnp.zeros((2 * C, 640), BF)
    high, rest = _split(both)
    emb = jnp.concatenate([emb_ref[...], next_ref[4 * C + 48 :]], axis=1)
    part = _dot_nt(emb, jnp.concatenate([none, high], axis=0)) + _dot_nt(
        emb, jnp.concatenate([none, rest], axis=0)
    )
    for i in range(4):
        value = jnp.where(at < 64, taps[4 * i + 1], taps[4 * i + 3])
        value = jnp.where((at & 63) < 32, jnp.where(at < 64, taps[4 * i], taps[4 * i + 2]), value)
        sums_ref[C * i : C * i + C] = value
    sums_ref[4 * C : 5 * C] = jnp.where(at < 32, taps[16], taps[17])
    sums_ref[5 * C : 9 * C] = pltpu.roll(part[: 4 * C], 64, 1) + part[4 * C :]
    sums_ref[9 * C :] = jnp.zeros((C, 128), F32)


def pair_field(total_bins, total_diags, *operands):
    vmem = pl.BlockSpec(memory_space=pltpu.VMEM)
    return pl.pallas_call(
        functools.partial(pair_kernel, total_bins, total_diags),
        out_shape=(
            jax.ShapeDtypeStruct((32, 384), F32),
            jax.ShapeDtypeStruct((2 * C, 384), F32),
            jax.ShapeDtypeStruct((C, 256), BF),
            jax.ShapeDtypeStruct((10 * C, 128), F32),
        ),
        in_specs=[pl.BlockSpec(memory_space=pltpu.SMEM)] * 2 + [vmem] * 7,
        out_specs=(vmem,) * 4,
        scratch_shapes=[
            pltpu.VMEM((3, 64 * C, LN), BF),
            pltpu.VMEM((3, 56 * C, LN), BF),
            pltpu.VMEM((3, 48 * C, LN), BF),
            pltpu.VMEM((3, 40 * C, LN), BF),
            pltpu.VMEM((64 * C, 384), F32),
            pltpu.VMEM((56 * C, LN), F32),
            pltpu.VMEM((40 * C, 384), F32),
            pltpu.VMEM((64, 8, LN), F32),
            pltpu.VMEM((C, 512), F32),
            pltpu.VMEM((C, 256), F32),
            pltpu.VMEM((C, LN), F32),
            pltpu.VMEM((48, LN), F32),
            pltpu.VMEM((6, 256, 512), F32),
            pltpu.VMEM((C, 384), F32),
            pltpu.VMEM((C, LN), F32),
        ],
        compiler_params=pltpu.CompilerParams(vmem_limit_bytes=42 * 2**20),
        cost_estimate=pl.CostEstimate(
            flops=12 * 10**9, bytes_accessed=5 * 10**6, transcendentals=3 * 10**6
        ),
        name="pair_field",
    )(*operands)


def finish_kernel(scaling, every_ref, proj_ref, conv_ref):
    diag_at = lax.axis_index("diag")
    row = pl.multiple_of((5 + (diag_at & 3)) * C, C)
    value = every_ref[pl.ds(row, C), :]
    proj_ref[...] = scaling * jnp.where(diag_at < 4, value[:, : 2 * C], value[:, 2 * C :])
    for tap in range(18):
        lanes = C * (tap % 4)
        value = every_ref[C * (tap // 4) : C * (tap // 4) + C, lanes : lanes + C]
        conv_ref[tap // 9, tap % 9] = scaling * value


def finish(scaling, every):
    vmem = pl.BlockSpec(memory_space=pltpu.VMEM)
    return pl.pallas_call(
        functools.partial(finish_kernel, scaling),
        out_shape=(
            jax.ShapeDtypeStruct((C, 2 * C), F32),
            jax.ShapeDtypeStruct((2, 9, C, C), F32),
        ),
        in_specs=[vmem],
        out_specs=(vmem, vmem),
        compiler_params=pltpu.CompilerParams(vmem_limit_bytes=16 * 2**20),
        name="finish",
    )(every)


def on_device(
    embeddings, projection, dist_bias, conv_weight, head_weight, dilations, band_limit, cotangent
):
    bins = lax.axis_size("bin")
    diags = lax.axis_size("diag")
    diag_dev, rows_dev = cotangent.shape
    total_bins = rows_dev * bins
    total_diags = diag_dev * diags
    diag_at = lax.axis_index("diag")
    first_diag = diag_at * diag_dev

    pack, cots = prepare(total_bins, diags, embeddings, projection, cotangent, band_limit)
    bands = band_weights(dilations, conv_weight)
    got = lax.all_to_all(pack, "diag", 0, 0)
    got, bands = lax.optimization_barrier((got, bands))
    columns = projection.shape[1]
    features = diag_dev * diags
    emb_all = got[:, :diag_dev].reshape(features, rows_dev)
    flat = got[:, diag_dev + 8 :]
    proj_all = jnp.concatenate(
        [flat[:, :, columns * i : columns * (i + 1)] for i in range(4)], axis=1
    ).reshape(features, columns)
    edges = got[:, diag_dev : diag_dev + 8]
    before = lax.dynamic_index_in_dim(edges, jnp.maximum(diag_at - 1, 0), 0, False)
    after = lax.dynamic_index_in_dim(edges, jnp.minimum(diag_at + 1, diags - 1), 0, False)
    before = jnp.where(diag_at > 0, before.astype(F32), 0.0)
    after = jnp.where(diag_at < diags - 1, after.astype(F32), 0.0)
    projected = lax.dot_general(
        proj_all, emb_all, (((0,), (0,)), ((), ())), preferred_element_type=F32
    )
    own = jnp.concatenate([projected, before, cots, after], axis=0)

    up = [(i, i + 1) for i in range(bins - 1)]
    down = [(i + 1, i) for i in range(bins - 1)]
    high, rest = _split(projected)
    first = jnp.concatenate(
        [
            high[C:, :256],
            rest[C:, :256],
            jnp.concatenate([high[C:, 256:], rest[C:, 256:]], axis=1),
            jnp.concatenate([high[:C, :128], rest[:C, :128]], axis=1),
            own[2 * C :, :256].astype(BF),
            emb_all[:, :256],
        ],
        axis=0,
    )
    nxt = lax.ppermute(first, "bin", down)
    prv = lax.ppermute(own[:, rows_dev - 128 :], "bin", up)

    predicted, both, spill, sums = pair_field(
        total_bins, total_diags, dilations, head_weight, nxt, prv, own, dist_bias, band_limit,
        bands, emb_all,
    )

    spill = lax.ppermute(spill, "bin", up)
    shares = lax.all_to_all(sums.reshape(bins, 10 * C // bins, 1, 128), "bin", 0, 0)
    both = both + jnp.pad(spill.astype(F32), ((C, 0), (0, rows_dev - spill.shape[1])))
    high, rest = _split(both)
    parts = _dot(
        jnp.concatenate([proj_all, proj_all], axis=1), jnp.concatenate([high, rest], axis=0)
    ).astype(BF).reshape(diags, diag_dev, rows_dev)
    share = jnp.sum(shares, axis=0)[:, 0]
    high, rest = _split(share)
    count = share.shape[0]
    tail = jnp.pad(jnp.concatenate([high, rest], axis=0), ((0, diag_dev - 2 * count), (0, 0)))
    parts = jnp.concatenate(
        [parts, jnp.broadcast_to(tail[None], (diags,) + tail.shape)], axis=2
    )
    total = jnp.sum(lax.all_to_all(parts, "diag", 0, 0).astype(F32), axis=0)
    grad_embed = total[:, :rows_dev]
    whole = total[:count, rows_dev:] + total[count : 2 * count, rows_dev:]
    every = lax.all_to_all(
        jnp.broadcast_to(whole[None, :, None], (bins, count, 1, 128)), "bin", 0, 0
    ).reshape(bins * count, 128)
    scaling = 1.0 / math.sqrt(total_bins * total_diags)
    grad_proj, grad_conv = finish(scaling, every)
    return (predicted, grad_embed, grad_proj, grad_conv)


def solution(mesh):
    return jax.shard_map(
        on_device,
        mesh=mesh,
        in_specs=(
            P("diag", "bin"),
            P("diag", None),
            P(),
            P(),
            P(),
            P(),
            P("bin"),
            P("diag", "bin"),
        ),
        out_specs=(P("diag", "bin"), P("diag", "bin"), P("diag", None), P()),
        check_vma=False,
    )
```

```python
import functools
import math

import jax
import jax.numpy as jnp
from jax import lax
from jax.experimental import pallas as pl
from jax.experimental.pallas import tpu as pltpu
from jax.sharding import PartitionSpec as P

C = 32
M = 16
LN = 512
BF = jnp.bfloat16
F32 = jnp.float32


def _dot(a, b):
    return jnp.dot(a, b, preferred_element_type=F32)


def _dot_nt(a, b):
    return lax.dot_general(a, b, (((1,), (1,)), ((), ())), preferred_element_type=F32)


def _split(x):
    hi = x.astype(BF)
    return hi, (x - hi.astype(F32)).astype(BF)


def band_kernel(dil_ref, w_ref, t_ref):
    lane = lax.broadcasted_iota(jnp.int32, (C, 384), 1)
    spread = ((lane & 31) == lax.broadcasted_iota(jnp.int32, (C, 384), 0)).astype(F32).astype(BF)
    offset = (lane >> 5) - 4
    for layer in range(2):
        step = dil_ref[layer]
        for kind in range(2):
            for slot in range(3):
                wide = []
                for b in range(3):
                    if kind == 0:
                        wide.append(_dot(w_ref[layer, 3 * slot + b], spread))
                    else:
                        w = w_ref[layer, 3 * (2 - slot) + 2 - b]
                        wide.append(
                            lax.dot_general(
                                w, spread, (((0,), (0,)), ((), ())), preferred_element_type=F32
                            )
                        )
                for j in range(4):
                    value = jnp.zeros((C, 384), F32)
                    for b in range(3):
                        value = jnp.where(offset == j + (b - 1) * step, wide[b], value)
                    t_ref[2 * kind + layer, C * j : C * j + C, 384 * slot : 384 * slot + 384] = (
                        value.astype(BF)
                    )


def band_weights(dilations, conv_weight):
    vmem = pl.BlockSpec(memory_space=pltpu.VMEM)
    return pl.pallas_call(
        band_kernel,
        out_shape=jax.ShapeDtypeStruct((4, 128, 1152), BF),
        in_specs=[pl.BlockSpec(memory_space=pltpu.SMEM), vmem],
        out_specs=vmem,
        compiler_params=pltpu.CompilerParams(vmem_limit_bytes=16 * 2**20),
        cost_estimate=pl.CostEstimate(flops=10**8, bytes_accessed=2 * 10**6, transcendentals=0),
        name="band_weights",
    )(dilations, conv_weight)


def prepare_kernel(
    total_bins, emb_hbm, proj_hbm, cot_hbm, limit_hbm, pack_ref, cots_ref,
    emb_ref, proj_ref, cot_ref, limit_ref, sems,
):
    copies = [
        pltpu.make_async_copy(source, target, sems.at[i])
        for i, (source, target) in enumerate(
            ((emb_hbm, emb_ref), (proj_hbm, proj_ref), (cot_hbm, cot_ref), (limit_hbm, limit_ref))
        )
    ]
    for copy in copies:
        copy.start()
    for copy in copies:
        copy.wait()
    diag_dev, rows_dev = cot_ref.shape
    diag_at = lax.axis_index("diag")
    first_row = lax.axis_index("bin") * rows_dev
    shape = (diag_dev, rows_dev)
    bin_id = first_row + lax.broadcasted_iota(jnp.int32, shape, 1)
    diag_id = diag_at * diag_dev + lax.broadcasted_iota(jnp.int32, shape, 0)
    counted = (bin_id + diag_id < total_bins) & (diag_id < limit_ref[...][None, :])
    cots = jnp.where(counted, cot_ref[...], 0.0)
    cots_ref[...] = cots
    columns = proj_ref.shape[1]
    quarter = diag_dev // 4
    proj = proj_ref[...].astype(F32)
    flat = jnp.concatenate(
        [proj[quarter * i : quarter * (i + 1)] for i in range(4)]
        + [jnp.zeros((quarter, rows_dev - 4 * columns), F32)],
        axis=1,
    )
    last = jnp.concatenate([cots[diag_dev - 8 :], flat], axis=0)
    first = jnp.concatenate([cots[:8], flat], axis=0)
    for peer in range(pack_ref.shape[0]):
        pack_ref[peer, :diag_dev] = emb_ref[...]
        pack_ref[peer, diag_dev:] = jnp.where(peer > diag_at, last, first).astype(BF)


def prepare(total_bins, diags, *operands):
    diag_dev, rows_dev = operands[0].shape
    vmem = pl.BlockSpec(memory_space=pltpu.VMEM)
    return pl.pallas_call(
        functools.partial(prepare_kernel, total_bins),
        out_shape=(
            jax.ShapeDtypeStruct((diags, diag_dev + 16, rows_dev), BF),
            jax.ShapeDtypeStruct((diag_dev, rows_dev), F32),
        ),
        in_specs=[pl.BlockSpec(memory_space=pltpu.HBM)] * 4,
        out_specs=(vmem, vmem),
        scratch_shapes=[pltpu.VMEM(x.shape, x.dtype) for x in operands]
        + [pltpu.SemaphoreType.DMA((4,))],
        compiler_params=pltpu.CompilerParams(vmem_limit_bytes=56 * 2**20),
        name="prepare",
    )(*operands)


def pair_kernel(
    total_bins, total_diags,
    dil_ref, head_ref, next_ref, prev_ref, own_ref, bias_ref, limit_ref, t_ref, emb_ref,
    pred_ref, both_ref, spill_ref, sums_ref,
    x0, x1, g2, g1, d0, d1, bk, mk, vbuf, ubuf, left, gwide, acc, lsum, rsum,
):
    first_row = lax.axis_index("bin") * 384
    first_diag = lax.axis_index("diag") * 32
    s1 = dil_ref[0]
    s2 = dil_ref[1]

    lane = lax.broadcasted_iota(jnp.int32, (8, LN), 1)
    low = lax.broadcasted_iota(jnp.int32, (C, 128), 1) < 64
    bin_id = first_row + jnp.where(lane < 448, lane, lane - LN)
    bin_ok = (bin_id >= 0) & (bin_id < total_bins)

    own = own_ref[...]
    prv = prev_ref[...]

    def rows_of(first, count, lanes):
        return next_ref[first : first + count, lanes].astype(F32)

    every, head_half, tail_half = slice(None), slice(0, 128), slice(128, 256)
    next_right = jnp.concatenate(
        [
            rows_of(0, C, every) + rows_of(C, C, every),
            rows_of(2 * C, C, head_half) + rows_of(2 * C, C, tail_half),
        ],
        axis=1,
    )
    next_left = rows_of(3 * C, C, head_half) + rows_of(3 * C, C, tail_half)
    next_cots = rows_of(4 * C, 48, head_half)
    left[:, :384] = own[:C]
    left[:, 384:] = jnp.where(low, next_left, prv[:C])
    low48 = lax.broadcasted_iota(jnp.int32, (48, 128), 1) < 64
    gwide[:, :384] = own[2 * C :]
    gwide[:, 384:] = jnp.where(low48, next_cots, prv[2 * C :])
    line = jnp.concatenate([prv[C : 2 * C], own[C : 2 * C], next_right], axis=1)
    bias = pltpu.roll(bias_ref[...], lax.rem(256 + M - first_diag, 256), 1)
    vbuf[...] = pltpu.roll(line, 784 - first_diag, 1)[:, :512]
    ubuf[...] = pltpu.roll(line, lax.rem(912 - first_diag, 896), 1)[:, :256]

    at = lax.broadcasted_iota(jnp.int32, (C, 128), 1)

    def spread(ref, rows, shift):
        for row in rows:
            cols = [ref[1, row : row + C, 128 * i : 128 * i + 128] for i in range(4)]
            later = [pltpu.roll(v, shift, 1) for v in cols]
            sooner = [pltpu.roll(v, 128 - shift, 1) for v in cols]
            for i in range(4):
                here = slice(128 * i, 128 * i + 128)
                ref[0, row : row + C, here] = jnp.where(at < shift, later[i - 1], later[i])
                ref[2, row : row + C, here] = jnp.where(
                    at < 128 - shift, sooner[i], sooner[(i + 1) % 4]
                )

    def times(value, mask):
        return (value.reshape(4, 8, value.shape[1]) * mask[None]).reshape(value.shape)

    def stage_zero(g, back):
        for r in range(8):
            k = 8 * g + r
            diag_id = first_diag - M + k
            ok = bin_ok & (bin_id + diag_id < total_bins) & (diag_id >= 0) & (diag_id < total_diags)
            mask = ok.astype(F32)
            mk[k] = mask
            by = (128 - k) % 128
            v = [pltpu.roll(vbuf[:, 128 * i : 128 * i + 128], by, 1) for i in range(4)]
            u = [pltpu.roll(ubuf[:, 128 * i : 128 * i + 128], by, 1) for i in range(2)]
            here = at < 128 - k
            shifted = jnp.concatenate(
                [jnp.where(here, v[i], v[i + 1]) for i in range(3)]
                + [jnp.where(low, v[3], jnp.where(here, u[0], u[1]))],
                axis=1,
            )
            t = jnp.tanh(left[...] + shifted + bias[:, k : k + 1])
            row = k * C
            x0[1, row : row + C] = times(t, mask).astype(BF)
            d0[pl.ds(row, C), :] = times(1.0 - t[:, :384] * t[:, :384], mask[:, :384])
        spread(x0, range(8 * g * C, (8 * g + 8) * C, C), s1)


    def window(ref, first, width):
        return [ref[a, first * C : (first + 12) * C, :width] for a in range(3)]

    def conv(kind, ref, first, width):
        return jnp.concatenate(
            [
                _dot(t_ref[kind], jnp.concatenate(window(ref, at_offset, width), axis=0))
                for at_offset in (first, first + 4)
            ],
            axis=0,
        )

    def stage_one(g, back):
        t1 = jnp.tanh(back)
        for r in range(8):
            k = 4 + 8 * g + r
            mask = mk[k]
            t = t1[r * C : (r + 1) * C]
            base = x0[1, pl.ds(k * C, C), :].astype(F32)
            x1[1, pl.ds((k - 4) * C, C), :] = times(base + t, mask).astype(BF)
            d1[pl.ds((k - 4) * C, C), :] = times(1.0 - t * t, mask)
        spread(x1, range(8 * g * C, (8 * g + 8) * C, C), s2)


    head = jnp.concatenate([jnp.full((1, LN), head_ref[c], F32) for c in range(C)], axis=0)
    limits = limit_ref[...][None, :]
    own_bin = first_row + lax.broadcasted_iota(jnp.int32, (8, 384), 1)
    own_row = lax.broadcasted_iota(jnp.int32, (8, 384), 0)

    def stage_two(g, back):
        t2 = jnp.tanh(back)
        cots = gwide[pl.ds(8 * g, 8), :]
        lines = []
        for r in range(8):
            k = 8 + 8 * g + r
            t = t2[r * C : (r + 1) * C]
            value = cots[r : r + 1] * (head * (1.0 - t * t))
            g2[1, pl.ds((k - 8) * C, C), :] = value.astype(BF)
            lines.append(jnp.sum(head[:, :384] * t[:, :384], axis=0, keepdims=True))
        spread(g2, range(8 * g * C, (8 * g + 8) * C, C), s2)

        if 1 <= g < 5:
            diag_id = first_diag + 8 * (g - 1) + own_row
            ok = (own_bin + diag_id < total_bins) & (diag_id < limits)
            pred_ref[pl.ds(8 * (g - 1), 8), :] = jnp.where(
                ok, jnp.concatenate(lines, axis=0), 0.0
            )


    def stage_three(g, back):
        for r in range(8):
            k = 12 + 8 * g + r
            value = back[r * C : (r + 1) * C]
            at = (k - 12) * C
            g1[1, pl.ds(at, C), :] = (value * d1[pl.ds((k - 4) * C, C), :]).astype(BF)
            bk[pl.ds(at, C), :] = times(value, mk[k])[:, :384]
        spread(g1, range(8 * g * C, (8 * g + 8) * C, C), s1)


    lsum[...] = jnp.zeros_like(lsum)
    rsum[...] = jnp.zeros_like(rsum)

    def stage_four(g, back):
        part = jnp.zeros((C, 384), F32)
        skew = jnp.zeros((C, LN), F32)
        for r in range(8):
            kk = 8 * g + r
            value = back[r * C : (r + 1) * C] + bk[pl.ds((kk + 4) * C, C), :]
            value = value * d0[pl.ds((kk + M) * C, C), :]
            part = part + value
            wide = jnp.concatenate([value, jnp.zeros((C, 128), F32)], axis=1)
            skew = skew + (pltpu.roll(wide, r, 1) if r else wide)
        lsum[...] += part
        rsum[...] += pltpu.roll(skew, 8 * g, 1)

    def wgrad(layer):
        grads, fields, shift, near_at = ((g1, x0, 4, 12), (g2, x1, 8, 8))[layer]
        lhs = jnp.concatenate([grads[1, (8 * g + shift) * C : (8 * g + shift + 8) * C, :384] for g in range(4)], axis=1)
        for a in range(3):
            rhs = jnp.concatenate([fields[a, (8 * g + near_at) * C : (8 * g + near_at + 16) * C, :384] for g in range(4)], axis=1)
            acc[3 * layer + a] = _dot_nt(lhs, rhs)

    stages = (
        (stage_zero, 8, None),
        (stage_one, 7, lambda g: conv(0, x0, 8 * g, LN)),
        (stage_two, 6, lambda g: conv(1, x1, 8 * g, LN)),
        (stage_three, 5, lambda g: conv(3, g2, 8 * g, LN)),
        (stage_four, 4, lambda g: conv(2, g1, 8 * g, 384)),
    )
    for stage, groups, dot in stages:
        for g in range(groups):
            stage(g, dot(g) if dot else None)
    wgrad(1)
    wgrad(0)
    rows = lax.broadcasted_iota(jnp.int32, (256, 512), 0) >> 5
    cols = lax.broadcasted_iota(jnp.int32, (256, 512), 1) >> 5
    delta = cols - rows - 4
    taps = []
    for layer in range(2):
        step = (s1, s2)[layer]
        for a in range(3):
            full = acc[3 * layer + a]
            for b in range(3):
                kept = jnp.where(delta == (b - 1) * step, full, 0.0)
                kept = jnp.sum(kept.reshape(8, C, 512), axis=0)
                kept = kept[:, :128] + kept[:, 128:256] + kept[:, 256:384] + kept[:, 384:]
                kept = kept + pltpu.roll(kept, 64, 1)
                taps.append(kept + pltpu.roll(kept, 32, 1))


    right = jnp.concatenate([rsum[...], jnp.zeros((C, 128), F32)], axis=1)
    right = pltpu.roll(right, first_diag, 1)
    both_ref[:C] = lsum[...]
    both_ref[C:] = right[:, :384]
    spill_ref[...] = right[:, 384:].astype(BF)
    both = jnp.concatenate(
        [jnp.concatenate([lsum[...], jnp.zeros((C, 256), F32)], axis=1), right], axis=0
    )
    none = jnp.zeros((2 * C, 640), BF)
    high, rest = _split(both)
    emb = jnp.concatenate([emb_ref[...], next_ref[4 * C + 48 :]], axis=1)
    part = _dot_nt(emb, jnp.concatenate([none, high], axis=0)) + _dot_nt(
        emb, jnp.concatenate([none, rest], axis=0)
    )
    blocks = []
    for i in range(4):
        value = jnp.where(at < 64, taps[4 * i + 1], taps[4 * i + 3])
        blocks.append(
            jnp.where((at & 63) < 32, jnp.where(at < 64, taps[4 * i], taps[4 * i + 2]), value)
        )
    blocks.append(jnp.where(at < 32, taps[16], taps[17]))
    value = pltpu.roll(part[: 4 * C], 64, 1) + part[4 * C :]
    blocks += [value[C * i : C * i + C] for i in range(4)] + [jnp.zeros((C, 128), F32)]
    sums_ref[...] = jnp.zeros_like(sums_ref)
    for t in range(5):
        sums_ref[pl.ds(t, 64, stride=8), :] = jnp.concatenate(blocks[2 * t : 2 * t + 2], axis=0)


def pair_field(total_bins, total_diags, *operands):
    vmem = pl.BlockSpec(memory_space=pltpu.VMEM)
    return pl.pallas_call(
        functools.partial(pair_kernel, total_bins, total_diags),
        out_shape=(
            jax.ShapeDtypeStruct((32, 384), F32),
            jax.ShapeDtypeStruct((2 * C, 384), F32),
            jax.ShapeDtypeStruct((C, 256), BF),
            jax.ShapeDtypeStruct((512, 128), F32),
        ),
        in_specs=[pl.BlockSpec(memory_space=pltpu.SMEM)] * 2 + [vmem] * 7,
        out_specs=(vmem,) * 4,
        scratch_shapes=[
            pltpu.VMEM((3, 64 * C, LN), BF),
            pltpu.VMEM((3, 56 * C, LN), BF),
            pltpu.VMEM((3, 48 * C, LN), BF),
            pltpu.VMEM((3, 40 * C, LN), BF),
            pltpu.VMEM((64 * C, 384), F32),
            pltpu.VMEM((56 * C, LN), F32),
            pltpu.VMEM((40 * C, 384), F32),
            pltpu.VMEM((64, 8, LN), F32),
            pltpu.VMEM((C, 512), F32),
            pltpu.VMEM((C, 256), F32),
            pltpu.VMEM((C, LN), F32),
            pltpu.VMEM((48, LN), F32),
            pltpu.VMEM((6, 256, 512), F32),
            pltpu.VMEM((C, 384), F32),
            pltpu.VMEM((C, LN), F32),
        ],
        compiler_params=pltpu.CompilerParams(vmem_limit_bytes=42 * 2**20),
        cost_estimate=pl.CostEstimate(
            flops=12 * 10**9, bytes_accessed=5 * 10**6, transcendentals=3 * 10**6
        ),
        name="pair_field",
    )(*operands)


def finish_kernel(scaling, every_ref, proj_ref, conv_ref):
    diag_at = lax.axis_index("diag")
    rows = [every_ref[pl.ds(t, 64, stride=5), :] for t in range(5)]
    blocks = [row[C * half : C * half + C] for row in rows for half in range(2)]
    value = blocks[5]
    for i in range(1, 4):
        value = jnp.where((diag_at & 3) == i, blocks[5 + i], value)
    proj_ref[...] = scaling * jnp.where(diag_at < 4, value[:, : 2 * C], value[:, 2 * C :])
    for tap in range(18):
        lanes = C * (tap % 4)
        conv_ref[tap // 9, tap % 9] = scaling * blocks[tap // 4][:, lanes : lanes + C]


def finish(scaling, every):
    vmem = pl.BlockSpec(memory_space=pltpu.VMEM)
    return pl.pallas_call(
        functools.partial(finish_kernel, scaling),
        out_shape=(
            jax.ShapeDtypeStruct((C, 2 * C), F32),
            jax.ShapeDtypeStruct((2, 9, C, C), F32),
        ),
        in_specs=[vmem],
        out_specs=(vmem, vmem),
        compiler_params=pltpu.CompilerParams(vmem_limit_bytes=16 * 2**20),
        name="finish",
    )(every)


def on_device(
    embeddings, projection, dist_bias, conv_weight, head_weight, dilations, band_limit, cotangent
):
    bins = lax.axis_size("bin")
    diags = lax.axis_size("diag")
    diag_dev, rows_dev = cotangent.shape
    total_bins = rows_dev * bins
    total_diags = diag_dev * diags
    diag_at = lax.axis_index("diag")
    first_diag = diag_at * diag_dev

    pack, cots = prepare(total_bins, diags, embeddings, projection, cotangent, band_limit)
    bands = band_weights(dilations, conv_weight)
    got = lax.all_to_all(pack, "diag", 0, 0)
    got, bands = lax.optimization_barrier((got, bands))
    columns = projection.shape[1]
    features = diag_dev * diags
    emb_all = got[:, :diag_dev].reshape(features, rows_dev)
    flat = got[:, diag_dev + 8 :]
    proj_all = jnp.concatenate(
        [flat[:, :, columns * i : columns * (i + 1)] for i in range(4)], axis=1
    ).reshape(features, columns)
    edges = got[:, diag_dev : diag_dev + 8]
    before = lax.dynamic_index_in_dim(edges, jnp.maximum(diag_at - 1, 0), 0, False)
    after = lax.dynamic_index_in_dim(edges, jnp.minimum(diag_at + 1, diags - 1), 0, False)
    before = jnp.where(diag_at > 0, before.astype(F32), 0.0)
    after = jnp.where(diag_at < diags - 1, after.astype(F32), 0.0)
    projected = lax.dot_general(
        proj_all, emb_all, (((0,), (0,)), ((), ())), preferred_element_type=F32
    )
    own = jnp.concatenate([projected, before, cots, after], axis=0)

    up = [(i, i + 1) for i in range(bins - 1)]
    down = [(i + 1, i) for i in range(bins - 1)]
    high, rest = _split(projected)
    first = jnp.concatenate(
        [
            high[C:, :256],
            rest[C:, :256],
            jnp.concatenate([high[C:, 256:], rest[C:, 256:]], axis=1),
            jnp.concatenate([high[:C, :128], rest[:C, :128]], axis=1),
            own[2 * C :, :256].astype(BF),
            emb_all[:, :256],
        ],
        axis=0,
    )
    nxt = lax.ppermute(first, "bin", down)
    prv = lax.ppermute(own[:, rows_dev - 128 :], "bin", up)

    predicted, both, spill, sums = pair_field(
        total_bins, total_diags, dilations, head_weight, nxt, prv, own, dist_bias, band_limit,
        bands, emb_all,
    )

    spill = lax.ppermute(spill, "bin", up)
    shares = lax.all_to_all(sums.reshape(bins, 512 // bins, 128), "bin", 0, 0)
    both = both + jnp.pad(spill.astype(F32), ((C, 0), (0, rows_dev - spill.shape[1])))
    high, rest = _split(both)
    parts = _dot(
        jnp.concatenate([proj_all, proj_all], axis=1), jnp.concatenate([high, rest], axis=0)
    ).astype(BF).reshape(diags, diag_dev, rows_dev)
    share = jnp.sum(shares, axis=0)[:5]
    high, rest = _split(share)
    count = share.shape[0]
    tail = jnp.pad(jnp.concatenate([high, rest], axis=0), ((0, diag_dev - 2 * count), (0, 0)))
    parts = jnp.concatenate(
        [parts, jnp.broadcast_to(tail[None], (diags,) + tail.shape)], axis=2
    )
    total = jnp.sum(lax.all_to_all(parts, "diag", 0, 0).astype(F32), axis=0)
    grad_embed = total[:, :rows_dev]
    whole = total[:count, rows_dev:] + total[count : 2 * count, rows_dev:]
    every = lax.all_to_all(
        jnp.broadcast_to(whole[None, :, None], (bins, count, 1, 128)), "bin", 0, 0
    ).reshape(bins * count, 128)
    scaling = 1.0 / math.sqrt(total_bins * total_diags)
    grad_proj, grad_conv = finish(scaling, every)
    return (predicted, grad_embed, grad_proj, grad_conv)


def solution(mesh):
    return jax.shard_map(
        on_device,
        mesh=mesh,
        in_specs=(
            P("diag", "bin"),
            P("diag", None),
            P(),
            P(),
            P(),
            P(),
            P("bin"),
            P("diag", "bin"),
        ),
        out_specs=(P("diag", "bin"), P("diag", "bin"), P("diag", None), P()),
        check_vma=False,
    )
```

```python
import functools
import math

import jax
import jax.numpy as jnp
from jax import lax
from jax.experimental import pallas as pl
from jax.experimental.pallas import tpu as pltpu
from jax.sharding import PartitionSpec as P

C = 32
M = 16
LN = 512
BF = jnp.bfloat16
F32 = jnp.float32


def _dot(a, b):
    return jnp.dot(a, b, preferred_element_type=F32)


def _dot_nt(a, b):
    return lax.dot_general(a, b, (((1,), (1,)), ((), ())), preferred_element_type=F32)


def _split(x):
    hi = x.astype(BF)
    return hi, (x - hi.astype(F32)).astype(BF)


def band_kernel(dil_ref, w_ref, t_ref):
    lane = lax.broadcasted_iota(jnp.int32, (C, 384), 1)
    spread = ((lane & 31) == lax.broadcasted_iota(jnp.int32, (C, 384), 0)).astype(F32).astype(BF)
    offset = (lane >> 5) - 4
    for layer in range(2):
        step = dil_ref[layer]
        for kind in range(2):
            for slot in range(3):
                wide = []
                for b in range(3):
                    if kind == 0:
                        wide.append(_dot(w_ref[layer, 3 * slot + b], spread))
                    else:
                        w = w_ref[layer, 3 * (2 - slot) + 2 - b]
                        wide.append(
                            lax.dot_general(
                                w, spread, (((0,), (0,)), ((), ())), preferred_element_type=F32
                            )
                        )
                for j in range(4):
                    value = jnp.zeros((C, 384), F32)
                    for b in range(3):
                        value = jnp.where(offset == j + (b - 1) * step, wide[b], value)
                    t_ref[2 * kind + layer, C * j : C * j + C, 384 * slot : 384 * slot + 384] = (
                        value.astype(BF)
                    )


def band_weights(dilations, conv_weight):
    vmem = pl.BlockSpec(memory_space=pltpu.VMEM)
    return pl.pallas_call(
        band_kernel,
        out_shape=jax.ShapeDtypeStruct((4, 128, 1152), BF),
        in_specs=[pl.BlockSpec(memory_space=pltpu.SMEM), vmem],
        out_specs=vmem,
        compiler_params=pltpu.CompilerParams(vmem_limit_bytes=16 * 2**20),
        cost_estimate=pl.CostEstimate(flops=10**8, bytes_accessed=2 * 10**6, transcendentals=0),
        name="band_weights",
    )(dilations, conv_weight)


def prepare_kernel(
    total_bins, emb_hbm, proj_hbm, cot_hbm, limit_hbm, pack_ref, cots_ref,
    emb_ref, proj_ref, cot_ref, limit_ref, sems,
):
    copies = [
        pltpu.make_async_copy(source, target, sems.at[i])
        for i, (source, target) in enumerate(
            ((emb_hbm, emb_ref), (proj_hbm, proj_ref), (cot_hbm, cot_ref), (limit_hbm, limit_ref))
        )
    ]
    for copy in copies:
        copy.start()
    for copy in copies:
        copy.wait()
    diag_dev, rows_dev = cot_ref.shape
    diag_at = lax.axis_index("diag")
    first_row = lax.axis_index("bin") * rows_dev
    shape = (diag_dev, rows_dev)
    bin_id = first_row + lax.broadcasted_iota(jnp.int32, shape, 1)
    diag_id = diag_at * diag_dev + lax.broadcasted_iota(jnp.int32, shape, 0)
    counted = (bin_id + diag_id < total_bins) & (diag_id < limit_ref[...][None, :])
    cots = jnp.where(counted, cot_ref[...], 0.0)
    cots_ref[...] = cots
    columns = proj_ref.shape[1]
    quarter = diag_dev // 4
    proj = proj_ref[...].astype(F32)
    flat = jnp.concatenate(
        [proj[quarter * i : quarter * (i + 1)] for i in range(4)]
        + [jnp.zeros((quarter, rows_dev - 4 * columns), F32)],
        axis=1,
    )
    last = jnp.concatenate([cots[diag_dev - 8 :], flat], axis=0)
    first = jnp.concatenate([cots[:8], flat], axis=0)
    for peer in range(pack_ref.shape[0]):
        pack_ref[peer, :diag_dev] = emb_ref[...]
        pack_ref[peer, diag_dev:] = jnp.where(peer > diag_at, last, first).astype(BF)


def prepare(total_bins, diags, *operands):
    diag_dev, rows_dev = operands[0].shape
    vmem = pl.BlockSpec(memory_space=pltpu.VMEM)
    return pl.pallas_call(
        functools.partial(prepare_kernel, total_bins),
        out_shape=(
            jax.ShapeDtypeStruct((diags, diag_dev + 16, rows_dev), BF),
            jax.ShapeDtypeStruct((diag_dev, rows_dev), F32),
        ),
        in_specs=[pl.BlockSpec(memory_space=pltpu.HBM)] * 4,
        out_specs=(vmem, vmem),
        scratch_shapes=[pltpu.VMEM(x.shape, x.dtype) for x in operands]
        + [pltpu.SemaphoreType.DMA((4,))],
        compiler_params=pltpu.CompilerParams(vmem_limit_bytes=56 * 2**20),
        name="prepare",
    )(*operands)


def pair_kernel(
    total_bins, total_diags,
    dil_ref, head_ref, next_ref, prev_ref, own_ref, bias_ref, limit_ref, t_ref, emb_ref,
    pred_ref, both_ref, spill_ref, sums_ref,
    x0, x1, g2, g1, d0, d1, bk, mk, vbuf, ubuf, left, gwide, acc, lsum, rsum,
):
    first_row = lax.axis_index("bin") * 384
    first_diag = lax.axis_index("diag") * 32
    s1 = dil_ref[0]
    s2 = dil_ref[1]

    lane = lax.broadcasted_iota(jnp.int32, (8, LN), 1)
    low = lax.broadcasted_iota(jnp.int32, (C, 128), 1) < 64
    bin_id = first_row + jnp.where(lane < 448, lane, lane - LN)
    bin_ok = (bin_id >= 0) & (bin_id < total_bins)

    own = own_ref[...]
    prv = prev_ref[...]

    def rows_of(first, count, lanes):
        return next_ref[first : first + count, lanes].astype(F32)

    every, head_half, tail_half = slice(None), slice(0, 128), slice(128, 256)
    next_right = jnp.concatenate(
        [
            rows_of(0, C, every) + rows_of(C, C, every),
            rows_of(2 * C, C, head_half) + rows_of(2 * C, C, tail_half),
        ],
        axis=1,
    )
    next_left = rows_of(3 * C, C, head_half) + rows_of(3 * C, C, tail_half)
    next_cots = rows_of(4 * C, 48, head_half)
    left[:, :384] = own[:C]
    left[:, 384:] = jnp.where(low, next_left, prv[:C])
    low48 = lax.broadcasted_iota(jnp.int32, (48, 128), 1) < 64
    gwide[:, :384] = own[2 * C :]
    gwide[:, 384:] = jnp.where(low48, next_cots, prv[2 * C :])
    line = jnp.concatenate([prv[C : 2 * C], own[C : 2 * C], next_right], axis=1)
    bias = pltpu.roll(bias_ref[...], lax.rem(256 + M - first_diag, 256), 1)
    vbuf[...] = pltpu.roll(line, 784 - first_diag, 1)[:, :512]
    ubuf[...] = pltpu.roll(line, lax.rem(912 - first_diag, 896), 1)[:, :256]

    at = lax.broadcasted_iota(jnp.int32, (C, 128), 1)

    def spread(ref, rows, shift):
        for row in rows:
            cols = [ref[1, row : row + C, 128 * i : 128 * i + 128] for i in range(4)]
            later = [pltpu.roll(v, shift, 1) for v in cols]
            sooner = [pltpu.roll(v, 128 - shift, 1) for v in cols]
            for i in range(4):
                here = slice(128 * i, 128 * i + 128)
                ref[0, row : row + C, here] = jnp.where(at < shift, later[i - 1], later[i])
                ref[2, row : row + C, here] = jnp.where(
                    at < 128 - shift, sooner[i], sooner[(i + 1) % 4]
                )

    def times(value, mask):
        return (value.reshape(4, 8, value.shape[1]) * mask[None]).reshape(value.shape)

    def stage_zero(g, back):
        for r in range(8):
            k = 8 * g + r
            diag_id = first_diag - M + k
            ok = bin_ok & (bin_id + diag_id < total_bins) & (diag_id >= 0) & (diag_id < total_diags)
            mask = ok.astype(F32)
            mk[k] = mask
            by = (128 - k) % 128
            v = [pltpu.roll(vbuf[:, 128 * i : 128 * i + 128], by, 1) for i in range(4)]
            u = [pltpu.roll(ubuf[:, 128 * i : 128 * i + 128], by, 1) for i in range(2)]
            here = at < 128 - k
            shifted = jnp.concatenate(
                [jnp.where(here, v[i], v[i + 1]) for i in range(3)]
                + [jnp.where(low, v[3], jnp.where(here, u[0], u[1]))],
                axis=1,
            )
            t = jnp.tanh(left[...] + shifted + bias[:, k : k + 1])
            row = k * C
            x0[1, row : row + C] = times(t, mask).astype(BF)
            d0[pl.ds(row, C), :] = times(1.0 - t[:, :384] * t[:, :384], mask[:, :384])
        spread(x0, range(8 * g * C, (8 * g + 8) * C, C), s1)


    def window(ref, first, width):
        return [ref[a, first * C : (first + 12) * C, :width] for a in range(3)]

    def conv(kind, ref, first, width):
        return jnp.concatenate(
            [
                _dot(t_ref[kind], jnp.concatenate(window(ref, at_offset, width), axis=0))
                for at_offset in (first, first + 4)
            ],
            axis=0,
        )

    def stage_one(g, back):
        t1 = jnp.tanh(back)
        for r in range(8):
            k = 4 + 8 * g + r
            mask = mk[k]
            t = t1[r * C : (r + 1) * C]
            base = x0[1, pl.ds(k * C, C), :].astype(F32)
            x1[1, pl.ds((k - 4) * C, C), :] = times(base + t, mask).astype(BF)
            d1[pl.ds((k - 4) * C, C), :] = times(1.0 - t * t, mask)
        spread(x1, range(8 * g * C, (8 * g + 8) * C, C), s2)


    head = jnp.concatenate([jnp.full((1, LN), head_ref[c], F32) for c in range(C)], axis=0)
    limits = limit_ref[...][None, :]
    own_bin = first_row + lax.broadcasted_iota(jnp.int32, (8, 384), 1)
    own_row = lax.broadcasted_iota(jnp.int32, (8, 384), 0)

    def stage_two(g, back):
        t2 = jnp.tanh(back)
        cots = gwide[pl.ds(8 * g, 8), :]
        lines = []
        for r in range(8):
            k = 8 + 8 * g + r
            t = t2[r * C : (r + 1) * C]
            value = cots[r : r + 1] * (head * (1.0 - t * t))
            g2[1, pl.ds((k - 8) * C, C), :] = value.astype(BF)
            lines.append(jnp.sum(head[:, :384] * t[:, :384], axis=0, keepdims=True))
        spread(g2, range(8 * g * C, (8 * g + 8) * C, C), s2)

        if 1 <= g < 5:
            diag_id = first_diag + 8 * (g - 1) + own_row
            ok = (own_bin + diag_id < total_bins) & (diag_id < limits)
            pred_ref[pl.ds(8 * (g - 1), 8), :] = jnp.where(
                ok, jnp.concatenate(lines, axis=0), 0.0
            )


    def stage_three(g, back):
        for r in range(8):
            k = 12 + 8 * g + r
            value = back[r * C : (r + 1) * C]
            at = (k - 12) * C
            g1[1, pl.ds(at, C), :] = (value * d1[pl.ds((k - 4) * C, C), :]).astype(BF)
            bk[pl.ds(at, C), :] = times(value, mk[k])[:, :384]
        spread(g1, range(8 * g * C, (8 * g + 8) * C, C), s1)


    lsum[...] = jnp.zeros_like(lsum)
    rsum[...] = jnp.zeros_like(rsum)

    def stage_four(g, back):
        part = jnp.zeros((C, 384), F32)
        skew = jnp.zeros((C, LN), F32)
        for r in range(8):
            kk = 8 * g + r
            value = back[r * C : (r + 1) * C] + bk[pl.ds((kk + 4) * C, C), :]
            value = value * d0[pl.ds((kk + M) * C, C), :]
            part = part + value
            wide = jnp.concatenate([value, jnp.zeros((C, 128), F32)], axis=1)
            skew = skew + (pltpu.roll(wide, r, 1) if r else wide)
        lsum[...] += part
        rsum[...] += pltpu.roll(skew, 8 * g, 1)

    def wgrad(layer):
        grads, fields, shift, near_at = ((g1, x0, 4, 12), (g2, x1, 8, 8))[layer]
        lhs = jnp.concatenate([grads[1, (8 * g + shift) * C : (8 * g + shift + 8) * C, :384] for g in range(4)], axis=1)
        for a in range(3):
            rhs = jnp.concatenate([fields[a, (8 * g + near_at) * C : (8 * g + near_at + 16) * C, :384] for g in range(4)], axis=1)
            acc[3 * layer + a] = _dot_nt(lhs, rhs)

    stages = (
        (stage_zero, 8, None),
        (stage_one, 7, lambda g: conv(0, x0, 8 * g, LN)),
        (stage_two, 6, lambda g: conv(1, x1, 8 * g, LN)),
        (stage_three, 5, lambda g: conv(3, g2, 8 * g, LN)),
        (stage_four, 4, lambda g: conv(2, g1, 8 * g, 384)),
    )
    for stage, groups, dot in stages:
        for g in range(groups):
            stage(g, dot(g) if dot else None)
    wgrad(1)
    wgrad(0)
    rows = lax.broadcasted_iota(jnp.int32, (256, 512), 0) >> 5
    cols = lax.broadcasted_iota(jnp.int32, (256, 512), 1) >> 5
    delta = cols - rows - 4
    taps = []
    for layer in range(2):
        step = (s1, s2)[layer]
        for a in range(3):
            full = acc[3 * layer + a]
            for b in range(3):
                kept = jnp.where(delta == (b - 1) * step, full, 0.0)
                kept = jnp.sum(kept.reshape(8, C, 512), axis=0)
                kept = kept[:, :128] + kept[:, 128:256] + kept[:, 256:384] + kept[:, 384:]
                kept = kept + pltpu.roll(kept, 64, 1)
                taps.append(kept + pltpu.roll(kept, 32, 1))


    right = jnp.concatenate([rsum[...], jnp.zeros((C, 128), F32)], axis=1)
    right = pltpu.roll(right, first_diag, 1)
    both_ref[:C] = lsum[...]
    both_ref[C:] = right[:, :384]
    spill_ref[...] = right[:, 384:].astype(BF)
    both = jnp.concatenate(
        [jnp.concatenate([lsum[...], jnp.zeros((C, 256), F32)], axis=1), right], axis=0
    )
    none = jnp.zeros((2 * C, 640), BF)
    high, rest = _split(both)
    emb = jnp.concatenate([emb_ref[...], next_ref[4 * C + 48 :]], axis=1)
    part = _dot_nt(emb, jnp.concatenate([none, high], axis=0)) + _dot_nt(
        emb, jnp.concatenate([none, rest], axis=0)
    )
    blocks = []
    for i in range(4):
        value = jnp.where(at < 64, taps[4 * i + 1], taps[4 * i + 3])
        blocks.append(
            jnp.where((at & 63) < 32, jnp.where(at < 64, taps[4 * i], taps[4 * i + 2]), value)
        )
    blocks.append(jnp.where(at < 32, taps[16], taps[17]))
    value = pltpu.roll(part[: 4 * C], 64, 1) + part[4 * C :]
    blocks += [value[C * i : C * i + C] for i in range(4)] + [jnp.zeros((C, 128), F32)]
    sums_ref[...] = jnp.zeros_like(sums_ref)
    for t in range(5):
        sums_ref[pl.ds(t, 64, stride=8), :] = jnp.concatenate(blocks[2 * t : 2 * t + 2], axis=0)


def pair_field(total_bins, total_diags, *operands):
    vmem = pl.BlockSpec(memory_space=pltpu.VMEM)
    return pl.pallas_call(
        functools.partial(pair_kernel, total_bins, total_diags),
        out_shape=(
            jax.ShapeDtypeStruct((32, 384), F32),
            jax.ShapeDtypeStruct((2 * C, 384), F32),
            jax.ShapeDtypeStruct((C, 256), BF),
            jax.ShapeDtypeStruct((512, 128), F32),
        ),
        in_specs=[pl.BlockSpec(memory_space=pltpu.SMEM)] * 2 + [vmem] * 7,
        out_specs=(vmem,) * 4,
        scratch_shapes=[
            pltpu.VMEM((3, 64 * C, LN), BF),
            pltpu.VMEM((3, 56 * C, LN), BF),
            pltpu.VMEM((3, 48 * C, LN), BF),
            pltpu.VMEM((3, 40 * C, LN), BF),
            pltpu.VMEM((64 * C, 384), F32),
            pltpu.VMEM((56 * C, LN), F32),
            pltpu.VMEM((40 * C, 384), F32),
            pltpu.VMEM((64, 8, LN), F32),
            pltpu.VMEM((C, 512), F32),
            pltpu.VMEM((C, 256), F32),
            pltpu.VMEM((C, LN), F32),
            pltpu.VMEM((48, LN), F32),
            pltpu.VMEM((6, 256, 512), F32),
            pltpu.VMEM((C, 384), F32),
            pltpu.VMEM((C, LN), F32),
        ],
        compiler_params=pltpu.CompilerParams(vmem_limit_bytes=42 * 2**20),
        cost_estimate=pl.CostEstimate(
            flops=12 * 10**9, bytes_accessed=5 * 10**6, transcendentals=3 * 10**6
        ),
        name="pair_field",
    )(*operands)


def combine_kernel(parts_ref, embed_ref, copies_ref):
    total = parts_ref[0].astype(F32)
    for peer in range(1, parts_ref.shape[0]):
        total = total + parts_ref[peer].astype(F32)
    columns = embed_ref.shape[1]
    embed_ref[...] = total[:, :columns]
    tail = total[:, columns:]
    place = lax.rem(lax.broadcasted_iota(jnp.int32, (40, 128), 0), 5)
    block = jnp.zeros((40, 128), F32)
    for row in range(5):
        block = jnp.where(place == row, tail[row : row + 1] + tail[row + 5 : row + 6], block)
    for i in range(copies_ref.shape[0] // 40):
        copies_ref[40 * i : 40 * i + 40] = block


def combine(bins, columns, parts):
    vmem = pl.BlockSpec(memory_space=pltpu.VMEM)
    return pl.pallas_call(
        combine_kernel,
        out_shape=(
            jax.ShapeDtypeStruct((parts.shape[1], columns), F32),
            jax.ShapeDtypeStruct((5 * bins, 128), F32),
        ),
        in_specs=[vmem],
        out_specs=(vmem, vmem),
        compiler_params=pltpu.CompilerParams(vmem_limit_bytes=16 * 2**20),
        name="combine",
    )(parts)


def finish_kernel(scaling, every_ref, proj_ref, conv_ref):
    diag_at = lax.axis_index("diag")
    rows = [every_ref[pl.ds(t, 64, stride=5), :] for t in range(5)]
    blocks = [row[C * half : C * half + C] for row in rows for half in range(2)]
    value = blocks[5]
    for i in range(1, 4):
        value = jnp.where((diag_at & 3) == i, blocks[5 + i], value)
    proj_ref[...] = scaling * jnp.where(diag_at < 4, value[:, : 2 * C], value[:, 2 * C :])
    for tap in range(18):
        lanes = C * (tap % 4)
        conv_ref[tap // 9, tap % 9] = scaling * blocks[tap // 4][:, lanes : lanes + C]


def finish(scaling, every):
    vmem = pl.BlockSpec(memory_space=pltpu.VMEM)
    return pl.pallas_call(
        functools.partial(finish_kernel, scaling),
        out_shape=(
            jax.ShapeDtypeStruct((C, 2 * C), F32),
            jax.ShapeDtypeStruct((2, 9, C, C), F32),
        ),
        in_specs=[vmem],
        out_specs=(vmem, vmem),
        compiler_params=pltpu.CompilerParams(vmem_limit_bytes=16 * 2**20),
        name="finish",
    )(every)


def on_device(
    embeddings, projection, dist_bias, conv_weight, head_weight, dilations, band_limit, cotangent
):
    bins = lax.axis_size("bin")
    diags = lax.axis_size("diag")
    diag_dev, rows_dev = cotangent.shape
    total_bins = rows_dev * bins
    total_diags = diag_dev * diags
    diag_at = lax.axis_index("diag")
    first_diag = diag_at * diag_dev

    pack, cots = prepare(total_bins, diags, embeddings, projection, cotangent, band_limit)
    bands = band_weights(dilations, conv_weight)
    got = lax.all_to_all(pack, "diag", 0, 0)
    got, bands = lax.optimization_barrier((got, bands))
    columns = projection.shape[1]
    features = diag_dev * diags
    emb_all = got[:, :diag_dev].reshape(features, rows_dev)
    flat = got[:, diag_dev + 8 :]
    proj_all = jnp.concatenate(
        [flat[:, :, columns * i : columns * (i + 1)] for i in range(4)], axis=1
    ).reshape(features, columns)
    edges = got[:, diag_dev : diag_dev + 8]
    before = lax.dynamic_index_in_dim(edges, jnp.maximum(diag_at - 1, 0), 0, False)
    after = lax.dynamic_index_in_dim(edges, jnp.minimum(diag_at + 1, diags - 1), 0, False)
    before = jnp.where(diag_at > 0, before.astype(F32), 0.0)
    after = jnp.where(diag_at < diags - 1, after.astype(F32), 0.0)
    projected = lax.dot_general(
        proj_all, emb_all, (((0,), (0,)), ((), ())), preferred_element_type=F32
    )
    own = jnp.concatenate([projected, before, cots, after], axis=0)

    up = [(i, i + 1) for i in range(bins - 1)]
    down = [(i + 1, i) for i in range(bins - 1)]
    high, rest = _split(projected)
    first = jnp.concatenate(
        [
            high[C:, :256],
            rest[C:, :256],
            jnp.concatenate([high[C:, 256:], rest[C:, 256:]], axis=1),
            jnp.concatenate([high[:C, :128], rest[:C, :128]], axis=1),
            own[2 * C :, :256].astype(BF),
            emb_all[:, :256],
        ],
        axis=0,
    )
    nxt = lax.ppermute(first, "bin", down)
    prv = lax.ppermute(own[:, rows_dev - 128 :], "bin", up)

    predicted, both, spill, sums = pair_field(
        total_bins, total_diags, dilations, head_weight, nxt, prv, own, dist_bias, band_limit,
        bands, emb_all,
    )

    spill = lax.ppermute(spill, "bin", up)
    shares = lax.all_to_all(sums.reshape(bins, 512 // bins, 128), "bin", 0, 0)
    both = both + jnp.pad(spill.astype(F32), ((C, 0), (0, rows_dev - spill.shape[1])))
    high, rest = _split(both)
    parts = _dot(
        jnp.concatenate([proj_all, proj_all], axis=1), jnp.concatenate([high, rest], axis=0)
    ).astype(BF).reshape(diags, diag_dev, rows_dev)
    share = jnp.sum(shares, axis=0)[:5]
    high, rest = _split(share)
    count = share.shape[0]
    tail = jnp.pad(jnp.concatenate([high, rest], axis=0), ((0, diag_dev - 2 * count), (0, 0)))
    parts = jnp.concatenate(
        [parts, jnp.broadcast_to(tail[None], (diags,) + tail.shape)], axis=2
    )
    grad_embed, copies = combine(bins, rows_dev, lax.all_to_all(parts, "diag", 0, 0))
    every = lax.all_to_all(copies.reshape(bins, count, 1, 128), "bin", 0, 0).reshape(bins * count, 128)
    scaling = 1.0 / math.sqrt(total_bins * total_diags)
    grad_proj, grad_conv = finish(scaling, every)
    return (predicted, grad_embed, grad_proj, grad_conv)


def solution(mesh):
    return jax.shard_map(
        on_device,
        mesh=mesh,
        in_specs=(
            P("diag", "bin"),
            P("diag", None),
            P(),
            P(),
            P(),
            P(),
            P("bin"),
            P("diag", "bin"),
        ),
        out_specs=(P("diag", "bin"), P("diag", "bin"), P("diag", None), P()),
        check_vma=False,
    )
```
